32 devices in a mesh: tm: 4 (over y, core), space: 8 (over z, x).
Axes of the slice: x: 2, y: 2, z: 4, core: 2. Of those that a mesh axis runs over, the one named last changes fastest.
Arguments:
- init_states: float32 [2, 4, 256, 16, 128], P(None, 'tm', None, 'space'), may hold values from -6 to 6
- forcing: float32 [2, 256, 16, 128], P(None, None, 'space'), may hold values from -6 to 6
- damp: float32 [2, 256, 16, 128], P(None, None, 'space'), may hold values from 0.3 to 0.95
- kappa_x: float32 [256], replicated, may hold values from 2 to 60
- kappa_y: float32 [16], replicated, may hold values from 2 to 60
- kappa_z: float32 [128], replicated, may hold values from 0.02 to 0.24
- sea_tiles: int32 [16, 1], replicated, may hold values 0 or 1
- phases: int32 [4], P('tm'), may hold values from 0 to 11
Outputs:
- slab_starts: float32 [2, 4, 256, 16, 128], P(None, 'tm', None, 'space')
The draws below stay inside these ranges and needn't reach their ends.
All inputs are finite; a program needn't handle non-finite values.
Results may differ from the reference program's by a relative error of at most 0.0003.
Values sent between devices are 32-bit elements; how exact they have to be, the bound alone decides.
A program may use at most 64 MiB of HBM per device.

```python
import math
import jax
import jax.numpy as jnp
from jax import lax

NX = 256
NY = 16
NZ = 128
TRACERS = 2
SLABS = 4
STEPS = 2
ITERS = 2
TILE = 16
PHASES = 12


def place_ends(values, key, smallest, largest):
    spot = [jax.random.randint(jax.random.fold_in(key, axis), (), 0, length) for axis, length in enumerate(values.shape)]
    longest = values.shape.index(max(values.shape))
    next_to = spot[:longest] + [(spot[longest] + 1) % values.shape[longest]] + spot[longest + 1:]
    return values.at[tuple(spot)].set(smallest).at[tuple(next_to)].set(largest)


def block_scale(stream_key, dims, split, low, high):
    level, own = 1.0, jax.random.fold_in(stream_key, 6)
    for axis_at, parts in split:
        draws = jnp.exp(jax.random.uniform(jax.random.fold_in(own, axis_at), (parts,), jnp.float32, low / len(split), high / len(split)))
        level = level * jnp.repeat(draws, dims[axis_at] // parts).reshape([-1 if axis == axis_at else 1 for axis in range(len(dims))])
    return level


def normal_values(key, dims, spread, reach, split=(), kind=jnp.bfloat16):
    loudness = block_scale(key, dims, split, -0.22, 0.18) if split else 1.0
    array = jax.random.normal(key, dims, jnp.float32) * spread * loudness
    return jnp.minimum(jnp.maximum(array, -reach), reach).astype(kind)


def setup_inputs(seed: int = 0) -> dict:
    seeds = jax.random.split(jax.random.key(seed), 9)
    init_states = normal_values(seeds[0], (TRACERS, SLABS, NX, NY, NZ), 1.0, 6.0, ((1, 4), (3, 8)), jnp.float32)
    forcing = normal_values(seeds[1], (TRACERS, NX, NY, NZ), 1.0, 6.0, ((2, 8),), jnp.float32)
    damp = jnp.clip(jnp.exp(math.log(0.95) - 1.1526795 * jax.random.uniform(seeds[2], (TRACERS, NX, NY, NZ), jnp.float32) ** block_scale(seeds[2], (TRACERS, NX, NY, NZ), ((2, 8),), -0.2, 0.2)), 0.3, 0.95)
    kappa_x = jnp.clip(jnp.exp(jax.random.uniform(seeds[3], (NX,), jnp.float32, math.log(2.0), math.log(60.0))), 2.0, 60.0)
    kappa_y = jnp.clip(jnp.exp(jax.random.uniform(seeds[4], (NY,), jnp.float32, math.log(2.0), math.log(60.0))), 2.0, 60.0)
    kappa_z = jnp.clip(jax.random.uniform(seeds[5], (NZ,), jnp.float32, 0.02, 0.24), 0.02, 0.24)
    sea_tiles = place_ends((jax.random.randint(seeds[6], (NX // TILE, NY // TILE), 0, 4) < 3).astype(jnp.int32), jax.random.fold_in(seeds[6], 1), 0, 1)
    phases = place_ends(jax.random.randint(seeds[7], (SLABS,), 0, PHASES), jax.random.fold_in(seeds[7], 1), 0, PHASES - 1).astype(jnp.int32)
    return dict(init_states=init_states, forcing=forcing, damp=damp, kappa_x=kappa_x, kappa_y=kappa_y, kappa_z=kappa_z, sea_tiles=sea_tiles, phases=phases)


def line_coefficients(kappa):
    face = 0.5 * (kappa[1:] + kappa[:-1])
    zero = jnp.zeros((1,), kappa.dtype)
    left = jnp.concatenate([zero, face])
    right = jnp.concatenate([face, zero])
    return (-left, 1.0 + left + right, -right)

def solve_lines(field, kappa):
    lower, middle, upper = line_coefficients(kappa)
    batch = field.shape[:-1]
    return lax.linalg.tridiagonal_solve(jnp.broadcast_to(lower, batch), jnp.broadcast_to(middle, batch), jnp.broadcast_to(upper, batch), field)

def solve_x(field, kappa_x):
    shape = field.shape
    flat = field.reshape(shape[0], shape[1], shape[2] * shape[3])
    return solve_lines(flat, kappa_x).reshape(shape)

def vertical_mix(field, kappa_z):
    face = 0.5 * (kappa_z[1:] + kappa_z[:-1])
    flux = face * (field[..., 1:] - field[..., :-1])
    zeros = jnp.zeros(field.shape[:-1] + (1,), field.dtype)
    flux = jnp.concatenate([zeros, flux, zeros], axis=-1)
    return field + flux[..., 1:] - flux[..., :-1]

def fine_map(field, phase, source, kappa_x, kappa_y, kappa_z):
    for step in range(STEPS):
        if step % 2 == 0:
            field = solve_lines(solve_x(field, kappa_x), kappa_y)
        else:
            field = solve_x(solve_lines(field, kappa_y), kappa_x)
        amplitude = jnp.cos(2.0 * math.pi * (phase * STEPS + step) / (PHASES * STEPS))
        field = vertical_mix(field, kappa_z) + amplitude * source
    return field

def reference(init_states, forcing, damp, kappa_x, kappa_y, kappa_z, sea_tiles, phases):
    tiles = sea_tiles.astype(jnp.float32)
    sea = jnp.repeat(jnp.repeat(tiles, TILE, axis=0), TILE, axis=1)
    source = forcing * sea[None, :, :, None]
    phase_float = phases.astype(jnp.float32)
    log_damp = jnp.log(damp)
    states = init_states
    for iteration in range(ITERS):
        starts = jnp.moveaxis(states, 1, 0)
        ends = lax.map(lambda item: fine_map(item[0], item[1], source, kappa_x, kappa_y, kappa_z), (starts, phase_float.reshape(SLABS, 1, 1, 1, 1)))
        factors = []
        offsets = []
        for slab in range(SLABS):
            weight = 1.0 + 0.5 * jnp.cos(2.0 * math.pi * phase_float[slab] / PHASES)
            factor = jnp.exp(weight * log_damp)
            factors.append(factor)
            offsets.append(ends[slab] - factor * starts[slab])
        product = jnp.ones_like(damp)
        total = jnp.zeros_like(damp)
        for slab in range(SLABS):
            product = factors[slab] * product
            total = factors[slab] * total + offsets[slab]
        first = total / (1.0 - product)
        fresh = [first]
        for slab in range(SLABS - 1):
            fresh.append(factors[slab] * fresh[-1] + offsets[slab])
        states = jnp.stack(fresh, axis=1)
    return states
```

```python
import functools
import math

import jax
import jax.numpy as jnp
from jax import lax
from jax.experimental import pallas as pl
from jax.experimental.pallas import tpu as pltpu
from jax.sharding import PartitionSpec as P

STEPS = 2
ITERS = 2
TILE = 16
PHASES = 12


def shifted(array, axis, by):
    devices = lax.axis_size(axis)
    return lax.ppermute(array, axis, [(i, (i + by) % devices) for i in range(devices)])


def line_inverse(kappa):
    face = 0.5 * (kappa[1:] + kappa[:-1])
    zero = jnp.zeros((1,), kappa.dtype)
    left = jnp.concatenate([zero, face])
    right = jnp.concatenate([face, zero])
    identity = jnp.eye(kappa.shape[0], dtype=kappa.dtype)
    return lax.linalg.tridiagonal_solve(-left, 1.0 + left + right, -right, identity)


def solve_lines(field, inverse):
    return jnp.matmul(inverse, field, precision=lax.Precision.HIGHEST)


def solve_x(field, inverse):
    shape = field.shape
    flat = field.reshape(shape[0], shape[1], shape[2], shape[3] * shape[4])
    return solve_lines(flat, inverse).reshape(shape)


def vertical_mix(field, kappa_z):
    face = 0.5 * (kappa_z[1:] + kappa_z[:-1])
    flux = face * (field[..., 1:] - field[..., :-1])
    zeros = jnp.zeros(field.shape[:-1] + (1,), field.dtype)
    flux = jnp.concatenate([zeros, flux, zeros], axis=-1)
    return field + flux[..., 1:] - flux[..., :-1]


def compose(earlier, later):
    return (earlier[0] * later[0], later[0] * earlier[1] + later[1])


def column_pass(field, inverse_y):
    return lax.all_to_all(
        solve_lines(
            lax.all_to_all(field, "space", split_axis=2, concat_axis=3, tiled=True), inverse_y
        ),
        "space",
        split_axis=3,
        concat_axis=2,
        tiled=True,
    )


def body(init_states, forcing, damp, kappa_x, kappa_y, kappa_z, sea_tiles, phases):
    row_count = init_states.shape[3]
    inverse_x = line_inverse(kappa_x)
    inverse_y = line_inverse(kappa_y)
    tiles = sea_tiles.astype(jnp.float32)
    sea = jnp.repeat(jnp.repeat(tiles, TILE, axis=0), TILE, axis=1)
    sea_rows = lax.dynamic_slice_in_dim(sea, lax.axis_index("space") * row_count, row_count, 1)
    source = (forcing * sea_rows[None, :, :, None])[:, None]
    phase_float = phases.astype(jnp.float32)
    weight = 1.0 + 0.5 * jnp.cos(2.0 * math.pi * phase_float / PHASES)
    factors = jnp.exp(weight[None, :, None, None, None] * jnp.log(damp)[:, None])
    states = init_states
    for iteration in range(ITERS):
        field = states
        for step in range(STEPS):
            amplitude = jnp.cos(2.0 * math.pi * (phase_float * STEPS + step) / (PHASES * STEPS))[
                None, :, None, None, None
            ]
            if step % 2 == 0:
                field = column_pass(solve_x(field, inverse_x), inverse_y)
            else:
                field = solve_x(column_pass(field, inverse_y), inverse_x)
            field = vertical_mix(field, kappa_z) + amplitude * source
        offsets = field - factors * states
        own_factor = factors[:, 0]
        own_offset = offsets[:, 0]
        own = (own_factor, own_offset)
        ident = (jnp.ones_like(own_factor), jnp.zeros_like(own_offset))
        count = lax.axis_size("tm")
        here = lax.axis_index("tm")
        lower_part = ident
        upper_part = ident
        moving = jnp.stack([own_factor, own_offset])
        for turn in range(1, count):
            moving = shifted(moving, "tm", 1)
            piece = (moving[0], moving[1])
            anchor = (here - turn) % count
            before = anchor < here
            joined_low = compose(piece, lower_part)
            joined_high = compose(piece, upper_part)
            lower_part = (
                jnp.where(before, joined_low[0], lower_part[0]),
                jnp.where(before, joined_low[1], lower_part[1]),
            )
            upper_part = (
                jnp.where(before, upper_part[0], joined_high[0]),
                jnp.where(before, upper_part[1], joined_high[1]),
            )
        period = compose(compose(lower_part, own), upper_part)
        first = period[1] / (1.0 - period[0])
        start = lower_part[0] * first + lower_part[1]
        fresh = [start]
        states = jnp.stack(fresh, axis=1)
    return states


LANES = 128
HALO = 2 * ITERS
MESH = pl.DeviceIdType.MESH


def dot(a, b):
    return jnp.dot(a, b, precision=lax.Precision.HIGHEST, preferred_element_type=jnp.float32)


def parts(a):
    high = a.astype(jnp.bfloat16)
    return high, (a - high.astype(jnp.float32)).astype(jnp.bfloat16)


def dot3(a, b):
    once = functools.partial(jnp.dot, preferred_element_type=jnp.float32)
    return once(a[0], b[0]) + (once(a[0], b[1]) + once(a[1], b[0]))


def iota(shape, axis):
    return lax.broadcasted_iota(jnp.int32, shape, axis)


def faces(kappa_row, n):
    row, col = iota((n, n), 0), iota((n, n), 1)
    own = jnp.sum(jnp.where(row == col, kappa_row, 0.0), axis=1, keepdims=True)
    face = 0.5 * (own + kappa_row)
    below = jnp.where(col == row - 1, face, 0.0)
    above = jnp.where(col == row + 1, face, 0.0)
    return (
        jnp.sum(below, axis=1, keepdims=True),
        jnp.sum(above, axis=1, keepdims=True),
        below + above,
    )


def reduced_inverse(kappa_row, n):
    lower, upper, _ = faces(kappa_row, n)
    shape = (n, LANES)
    a = jnp.broadcast_to(-lower, shape)
    c = jnp.broadcast_to(-upper, shape)
    b = 1.0 - a - c
    blocks = [
        (iota(shape, 0) == iota(shape, 1) + LANES * j).astype(jnp.float32)
        for j in range(max(n // LANES, 1))
    ]
    s = 1
    while s < n:
        before = functools.partial(pltpu.roll, shift=s, axis=0)
        after = functools.partial(pltpu.roll, shift=n - s, axis=0)
        alpha = -a / before(b)
        gamma = -c / after(b)
        blocks = [d + alpha * before(d) + gamma * after(d) for d in blocks]
        b = b + alpha * before(c) + gamma * after(a)
        a, c = alpha * before(a), gamma * after(c)
        s *= 2
    inverse = 1.0 / b
    return [d * inverse for d in blocks]


def copied(pick, a):
    high, low = parts(a)
    once = functools.partial(jnp.dot, preferred_element_type=jnp.float32)
    return once(pick, high) + once(pick, low)


def spread(a, pick):
    high, low = parts(a)
    once = functools.partial(jnp.dot, preferred_element_type=jnp.float32)
    return once(high, pick) + once(low, pick)


def period_kernel(
    size, u_hbm, f_hbm, damp_hbm, kx_hbm, ky_hbm, kz_hbm, sea_hbm, phase_ref, out_ref,
    u_ref, f_ref, damp_ref, kx_ref, ky_ref, kz_ref, sea_ref, fetched, inverse_p,
    g_split, a_split, g_ref, a_ref, w_high, w_low, ends,
    ubuf, fbuf, pbuf, xbuf, dbuf, qbuf, obuf, rbuf, state, factor, source, offset_ref,
    near_out, near_in, last_out, last_in,
    u_send, u_recv, f_send, f_recv, p_send, p_recv, o_send, o_recv,
    near_send, near_recv, last_send, last_recv,
):
    n_tm, n_sp, n_t, nx, rows, nz = size
    spots = n_sp // 2
    count = n_tm * spots
    per = count // n_t
    chunk = nz // per
    window = chunk + 2 * HALO
    halves = nx // LANES
    wrows = window * rows
    crows = chunk * rows
    all_rows = spots * wrows
    tail, kept = 2 * chunk, 2 * (chunk + HALO)
    ext = LANES * -(-(all_rows + kept) // LANES)
    ny = n_sp * rows

    here = lax.axis_index("tm")
    space = lax.axis_index("space")
    side, spot = space // spots, space % spots
    me = here * spots + spot
    across = {"tm": here, "space": (1 - side) * spots + spot}

    def window_start(k):
        return jnp.minimum(jnp.maximum(k * chunk - HALO, 0), nz - window)

    def window_rows(k):
        return pl.ds(pl.multiple_of(window_start(k) * rows, 8), wrows)

    def chunk_rows(k):
        return pl.ds(pl.multiple_of(k * crows, 8), crows)

    def device(index):
        return {"tm": index // spots, "space": side * spots + index % spots}

    pairs = (
        (u_hbm, u_ref),
        (f_hbm, f_ref),
        (damp_hbm, damp_ref),
        (kx_hbm, kx_ref),
        (ky_hbm, ky_ref),
        (kz_hbm, kz_ref),
        (sea_hbm, sea_ref),
    )
    fetches = [
        pltpu.make_async_copy(far, near, fetched.at[i]) for i, (far, near) in enumerate(pairs)
    ]
    for fetch in fetches:
        fetch.start()

    barrier = pltpu.get_barrier_semaphore()

    @pl.loop(1, count)
    def greet(offset):
        pl.semaphore_signal(
            barrier, inc=1, device_id=device((me + offset) % count), device_id_type=MESH
        )

    pl.semaphore_signal(barrier, inc=1, device_id=across, device_id_type=MESH)

    def turn(ref, buf, where):
        for t in range(n_t):
            for half in range(halves):
                for y in range(rows):
                    part = ref[t, pl.ds(half * LANES * rows + y, LANES, stride=rows), :]
                    buf[(t, *where, half, pl.ds(y, nz, stride=rows), slice(None))] = part.T

    pbuf[...] = jnp.full((8, LANES), phase_ref[0].astype(jnp.float32))

    my_t, my_k = me // per, me % per
    my_start = window_start(my_k)

    own_u = pltpu.make_async_copy(
        ubuf.at[my_t, :, window_rows(my_k), :], xbuf.at[here, spot], u_recv.at[me]
    )
    own_f = [
        pltpu.make_async_copy(
            fbuf.at[my_t, which, :, window_rows(my_k), :],
            dbuf.at[which, spot],
            f_recv.at[which, spot],
        )
        for which in range(2)
    ]
    own_p = pltpu.make_async_copy(pbuf, qbuf.at[here], p_recv.at[here])

    def send_u(offset):
        index = (me + offset) % count
        return pltpu.make_async_remote_copy(
            src_ref=ubuf.at[index // per, :, window_rows(index % per), :],
            dst_ref=xbuf.at[here, spot],
            send_sem=u_send.at[offset],
            recv_sem=u_recv.at[me],
            device_id=device(index),
            device_id_type=MESH,
        )

    def send_f(which, offset):
        index = here * spots + (spot + offset) % spots
        return pltpu.make_async_remote_copy(
            src_ref=fbuf.at[index // per, which, :, window_rows(index % per), :],
            dst_ref=dbuf.at[which, spot],
            send_sem=f_send.at[which, offset],
            recv_sem=f_recv.at[which, spot],
            device_id=device(index),
            device_id_type=MESH,
        )

    def send_p(offset):
        return pltpu.make_async_remote_copy(
            src_ref=pbuf,
            dst_ref=qbuf.at[here],
            send_sem=p_send.at[offset],
            recv_sem=p_recv.at[here],
            device_id={"tm": (here + offset) % n_tm, "space": space},
            device_id_type=MESH,
        )

    def send_near(n):
        return pltpu.make_async_remote_copy(
            src_ref=near_out.at[n],
            dst_ref=near_in.at[n],
            send_sem=near_send.at[n],
            recv_sem=near_recv.at[n],
            device_id=across,
            device_id_type=MESH,
        )

    def send_last(n, half):
        return pltpu.make_async_remote_copy(
            src_ref=last_out.at[n, half],
            dst_ref=last_in.at[n, half],
            send_sem=last_send.at[n, half],
            recv_sem=last_recv.at[n, half],
            device_id=across,
            device_id_type=MESH,
        )

    def send_o(half, index):
        return pltpu.make_async_remote_copy(
            src_ref=obuf.at[half, index // spots, index % spots],
            dst_ref=rbuf.at[half, my_t, chunk_rows(my_k), :],
            send_sem=o_send.at[half, index],
            recv_sem=o_recv.at[half, me],
            device_id=device(index),
            device_id_type=MESH,
        )

    fetches[0].wait()
    turn(u_ref, ubuf, ())
    pl.semaphore_wait(barrier, count)

    @pl.loop(1, n_tm)
    def start_p(offset):
        send_p(offset).start()

    @pl.loop(1, count // 2 + 1)
    def start_u(offset):
        send_u(offset).start()

    own_p.start()
    own_u.start()
    fetches[1].wait()
    turn(f_ref, fbuf, (0,))

    @pl.loop(1, spots)
    def start_f(offset):
        send_f(0, offset).start()

    own_f[0].start()

    @pl.loop(count // 2 + 1, count)
    def start_u_rest(offset):
        send_u(offset).start()

    fetches[2].wait()
    turn(damp_ref, fbuf, (1,))

    @pl.loop(1, spots)
    def start_damp(offset):
        send_f(1, offset).start()

    own_f[1].start()
    for fetch in fetches[3:]:
        fetch.wait()

    for half, block in enumerate(reduced_inverse(kx_ref[...], nx)):
        a_ref[:, half * LANES : (half + 1) * LANES] = block
    a_once = a_ref[...]
    for i, part in enumerate(parts(a_once)):
        a_split[0, i] = part
    for i, part in enumerate(parts(dot(a_once, a_once))):
        a_split[1, i] = part

    inverse_y = reduced_inverse(ky_ref[...], ny)[0]
    row, col = iota((ny, LANES), 0), iota((ny, LANES), 1)
    edge, far_edge = ny // 2 - 1 + side, ny // 2 - side
    own_row, own_col = row // (ny // 2) == side, col // (ny // 2) == side
    inner_y = jnp.where(own_row & own_col, inverse_y, 0.0)
    twice_y = dot(inverse_y[:, :ny], inverse_y)
    inner_twice = dot(inner_y[:, :ny], inner_y)
    corner = jnp.sum(
        jnp.sum(
            jnp.where((row == far_edge) & (col == far_edge), inverse_y, 0.0), axis=1, keepdims=True
        ),
        axis=0,
        keepdims=True,
    )
    leave_once = jnp.sum(jnp.where(row == edge, inner_y, 0.0), axis=0, keepdims=True)
    leave_twice = jnp.sum(jnp.where(row == edge, inner_twice, 0.0), axis=0, keepdims=True)
    enter_line = (
        jnp.sum(jnp.where((row == far_edge) & own_col, inverse_y, 0.0), axis=0, keepdims=True)
        / corner
    )
    enter_once = (
        jnp.sum(jnp.where((col == far_edge) & own_row, inverse_y, 0.0), axis=1, keepdims=True)
        / corner
    )
    enter_twice = jnp.sum(inner_y * enter_line, axis=1, keepdims=True)
    below = iota((ny, LANES), 0)
    ext_y_once = jnp.concatenate(
        [
            inverse_y + jnp.where(col == ny, enter_once, 0.0),
            jnp.where(below == 0, leave_once, 0.0),
        ],
        axis=0,
    )
    ext_y_twice = jnp.concatenate(
        [
            twice_y
            + jnp.where(col == ny, enter_twice, 0.0)
            + jnp.where(col == ny + 1, enter_once, 0.0),
            jnp.where(below == 0, leave_once, jnp.where(below == 1, leave_twice, 0.0)),
        ],
        axis=0,
    )

    def line_of(q):
        own = side * (ny // 2) + (q // wrows) * rows + q % rows
        return jnp.where(q < all_rows, own, ny + q % 2)

    def level_of(q):
        own = my_start + (q % wrows) // rows
        p = (q - all_rows) // 2
        first = my_k * chunk
        ring = jnp.where(p < chunk + HALO // 2, first - HALO // 2 - chunk, first - HALO // 2) + p
        passed = jnp.where(p < chunk, first + p, ring)
        return jnp.where(q < all_rows, own, jnp.where(q < all_rows + kept, passed, -1))

    def mask(a, b):
        return jnp.where(a == b, 1.0, 0.0).astype(jnp.bfloat16)

    pick_y = mask(line_of(iota((ext, 2 * ny), 0)), iota((ext, 2 * ny), 1))
    pick_y_back = mask(line_of(iota((LANES, ext), 1)), iota((LANES, ext), 0))
    pick_z = mask(level_of(iota((ext, nz), 0)), iota((ext, nz), 1))
    pick_z_back = mask(level_of(iota((nz, ext), 1)), iota((nz, ext), 0))
    own_columns = iota((nz, ext), 1) < all_rows
    _, _, beside = faces(kz_ref[...], nz)
    identity = (iota((nz, nz), 0) == iota((nz, nz), 1)).astype(jnp.float32)
    vertical = beside + identity * (1.0 - jnp.sum(beside, axis=1, keepdims=True))
    for order, (ext_y, mixed) in enumerate(
        ((ext_y_once, vertical), (ext_y_twice, dot(vertical, vertical)))
    ):
        across_y = spread(copied(pick_y, ext_y), pick_y_back)
        levels = jnp.where(own_columns, spread(mixed, pick_z_back), pick_z_back.astype(jnp.float32))
        whole = across_y * copied(pick_z, levels)
        for i, part in enumerate(parts(whole)):
            g_split[order, i] = part
    g_ref[...] = whole
    inner = (my_k * chunk - my_start) * rows

    def inner_rows(r):
        return pl.ds(pl.multiple_of(r * wrows + inner, 8), crows)

    for i, part in enumerate(
        parts(jnp.concatenate([g_ref[inner_rows(r), :] for r in range(spots)], axis=0))
    ):
        g_split[2, i, : spots * crows, :] = part

    w_high[:, all_rows:, :] = jnp.zeros((n_tm + 1, ext - all_rows, nx), jnp.bfloat16)
    w_low[:, all_rows:, :] = jnp.zeros((n_tm + 1, ext - all_rows, nx), jnp.bfloat16)

    tile = (iota((nx // TILE, nx), 1) // TILE == iota((nx // TILE, nx), 0)).astype(jnp.float32)
    tiles = nx // TILE
    flags = jnp.where(
        iota((tiles, tiles), 0) == iota((tiles, tiles), 1), sea_ref[...].astype(jnp.float32), 0.0
    )
    sea = jnp.sum(jnp.sum(flags, axis=1, keepdims=True) * tile, axis=0, keepdims=True)

    def gathered(ref, where):
        return jnp.concatenate(
            [ref[where(half)].reshape(all_rows, LANES) for half in range(halves)], axis=1
        )

    def solve_x_lines(n, order, field):
        moved = dot3(parts(field), (a_split[order, 0], a_split[order, 1]))
        w_high[n, :all_rows, :], w_low[n, :all_rows, :] = parts(moved)

    def leaving(n, order, lines):
        padded = 16 * -(-lines // 16)
        block = slice(all_rows, all_rows + padded)
        found = dot3(
            (g_split[order, 0, block, :], g_split[order, 1, block, :]), (w_high[n], w_low[n])
        )
        return found[:lines]

    def joined(n, order):
        w_high[n, all_rows:, :], w_low[n, all_rows:, :] = parts(
            jnp.concatenate(
                [near_in[n], jnp.zeros((ext - all_rows - kept, nx), jnp.float32)], axis=0
            )
        )
        block = slice(0, all_rows)
        return dot3(
            (g_split[order, 0, block, :], g_split[order, 1, block, :]), (w_high[n], w_low[n])
        )

    def arrive_u(turned):
        n = (here + n_tm - turned) % n_tm

        @pl.loop(0, spots)
        def wait_u(r):
            slot = xbuf.at[n, r]
            pltpu.make_async_copy(slot, slot, u_recv.at[n * spots + r]).wait()

        solve_x_lines(n, 1, gathered(xbuf, lambda half: (n, slice(None), half)))
        near_out[n] = leaving(n, 1, kept)
        send_near(n).start()

    pl.loop(1, n_tm // 2 + 1)(arrive_u)

    @pl.loop(0, spots)
    def wait_f(r):
        slot = dbuf.at[0, r]
        pltpu.make_async_copy(slot, slot, f_recv.at[0, r]).wait()

    source[1] = gathered(dbuf, lambda half: (0, slice(None), half)) * sea
    solve_x_lines(n_tm, 0, source[1])
    near_out[n_tm] = leaving(n_tm, 0, kept)
    send_near(n_tm).start()

    pl.loop(n_tm // 2 + 1, n_tm + 1)(arrive_u)

    @pl.loop(0, n_tm)
    def wait_p(n):
        pltpu.make_async_copy(qbuf.at[n], qbuf.at[n], p_recv.at[n]).wait()

    @pl.loop(0, spots)
    def wait_damp(r):
        slot = dbuf.at[1, r]
        pltpu.make_async_copy(slot, slot, f_recv.at[1, r]).wait()

    def wide(values):
        return jnp.concatenate([values[:1]] * halves, axis=1)

    log_damp = jnp.log(gathered(dbuf, lambda half: (1, slice(None), half)))
    product = None
    for n in range(n_tm):
        weight = 1.0 + 0.5 * jnp.cos(2.0 * math.pi * qbuf[n] / PHASES)
        one = jnp.exp(wide(weight) * log_damp)
        factor[n] = one
        product = one if product is None else one * product
    inverse_p[...] = 1.0 / (1.0 - product)

    def wait_near(n):
        pltpu.make_async_copy(near_in.at[n], near_in.at[n], near_recv.at[n]).wait()

    wait_near(n_tm)
    source[0] = joined(n_tm, 0)

    @pl.loop(0, n_tm)
    def make_offsets(n):
        phase = qbuf[n]
        first = jnp.cos(2.0 * math.pi * (phase * STEPS) / (PHASES * STEPS))
        second = jnp.cos(2.0 * math.pi * (phase * STEPS + 1) / (PHASES * STEPS))
        offset_ref[n] = wide(first) * source[0] + wide(second) * source[1]

    @pl.loop(1, n_tm + 1)
    def finish_first(turned):
        n = (here + n_tm - turned) % n_tm
        wait_near(n)
        field = gathered(xbuf, lambda half: (n, slice(None), half))
        state[n] = joined(n, 1) + offset_ref[n] - factor[n] * field

    @pl.loop(0, spots)
    def solve_first(r):
        block = pl.ds(pl.multiple_of(r * wrows, 8), wrows)
        factors = [factor[n, block, :] for n in range(n_tm)]
        offsets = [state[n, block, :] for n in range(n_tm)]
        total = offsets[0]
        for n in range(1, n_tm):
            total = factors[n] * total + offsets[n]
        fresh = total * inverse_p[block, :]
        for n in range(n_tm):
            state[n, block, :] = fresh
            fresh = factors[n] * fresh + offsets[n]

    def lanes(half):
        return slice(half * LANES, (half + 1) * LANES)

    @pl.loop(0, n_tm)
    def leave_last(n):
        solve_x_lines(n, 1, state[n])
        found = leaving(n, 1, tail)
        for half in range(halves):
            last_out[n, half] = found[:, lanes(half)]
        send_last(n, 0).start()

    for half in range(1, halves):

        @pl.loop(0, n_tm)
        def start_last(n):
            send_last(n, half).start()

    for half in range(halves):

        @pl.loop(0, n_tm)
        def finish_last(n):
            slot = last_in.at[n, half]
            pltpu.make_async_copy(slot, slot, last_recv.at[n, half]).wait()
            block = slice(all_rows, all_rows + tail)
            high, low = parts(last_in[n, half])
            w_high[n, block, lanes(half)] = high
            w_low[n, block, lanes(half)] = low
            upper = slice(0, spots * crows)
            ends[n] = dot3(
                (g_split[2, 0, upper, :], g_split[2, 1, upper, :]),
                (w_high[n, :, lanes(half)], w_low[n, :, lanes(half)]),
            )

        @pl.loop(1, spots + 1)
        def solve_last(turned):
            r = (spot + turned) % spots
            block = inner_rows(r)
            packed = pl.ds(pl.multiple_of(r * crows, 8), crows)
            factors = [factor[n, block, lanes(half)] for n in range(n_tm)]
            offsets = [
                ends[n, packed, :]
                + offset_ref[n, block, lanes(half)]
                - factors[n] * state[n, block, lanes(half)]
                for n in range(n_tm)
            ]
            total = offsets[0]
            for n in range(1, n_tm):
                total = factors[n] * total + offsets[n]
            fresh = total * inverse_p[block, lanes(half)]
            for n in range(n_tm):
                obuf[half, n, r] = fresh
                fresh = factors[n] * fresh + offsets[n]
            for n in range(n_tm):

                @pl.when(n * spots + r != me)
                def _():
                    send_o(half, n * spots + r).start()

        pltpu.make_async_copy(
            obuf.at[half, here, spot], rbuf.at[half, my_t, chunk_rows(my_k), :], o_recv.at[half, me]
        ).start()

    for half in range(halves):
        for t in range(n_t):

            @pl.loop(t * per, (t + 1) * per)
            def wait_o(index):
                slot = rbuf.at[half, t, chunk_rows(index % per), :]
                pltpu.make_async_copy(slot, slot, o_recv.at[half, index]).wait()

            for y in range(rows):
                part = rbuf[half, t, pl.ds(y, nz, stride=rows), :]
                out_ref[t, pl.ds(half * LANES * rows + y, LANES, stride=rows), :] = part.T

    @pl.loop(1, count)
    def sent(offset):
        send_u(offset).wait_send()
        for half in range(halves):
            send_o(half, (me + offset) % count).wait_send()

    @pl.loop(1, spots)
    def sent_f(offset):
        for which in range(2):
            send_f(which, offset).wait_send()

    @pl.loop(1, n_tm)
    def sent_p(offset):
        send_p(offset).wait_send()

    @pl.loop(0, n_tm + 1)
    def sent_near(n):
        send_near(n).wait_send()

    @pl.loop(0, n_tm)
    def sent_last(n):
        for half in range(halves):
            send_last(n, half).wait_send()


def whole_period(init_states, forcing, damp, kappa_x, kappa_y, kappa_z, sea_tiles, phases):
    n_tm, n_sp = lax.axis_size("tm"), lax.axis_size("space")
    n_t, _, nx, rows, nz = init_states.shape
    spots = n_sp // 2
    count = n_tm * spots
    chunk = nz // (count // n_t)
    window = chunk + 2 * HALO
    halves = nx // LANES
    wrows = window * rows
    crows = chunk * rows
    all_rows = spots * wrows
    tail, kept = 2 * chunk, 2 * (chunk + HALO)
    ext = LANES * -(-(all_rows + kept) // LANES)
    flat = (n_t, nx * rows, nz)
    vmem = pl.BlockSpec(memory_space=pltpu.VMEM)
    f32 = jnp.float32
    bf16 = jnp.bfloat16
    out = pl.pallas_call(
        functools.partial(period_kernel, (n_tm, n_sp, n_t, nx, rows, nz)),
        out_shape=jax.ShapeDtypeStruct(flat, f32),
        in_specs=[pl.BlockSpec(memory_space=pltpu.HBM)] * 7 + [pl.BlockSpec(memory_space=pltpu.SMEM)],
        out_specs=vmem,
        scratch_shapes=[
            pltpu.VMEM(flat, f32),
            pltpu.VMEM(flat, f32),
            pltpu.VMEM(flat, f32),
            pltpu.VMEM((1, nx), f32),
            pltpu.VMEM((1, kappa_y.shape[0]), f32),
            pltpu.VMEM((1, nz), f32),
            pltpu.VMEM((1, sea_tiles.shape[0]), jnp.int32),
            pltpu.SemaphoreType.DMA((7,)),
            pltpu.VMEM((all_rows, nx), f32),
            pltpu.VMEM((3, 2, ext, ext), bf16),
            pltpu.VMEM((2, 2, nx, nx), bf16),
            pltpu.VMEM((ext, ext), f32),
            pltpu.VMEM((nx, nx), f32),
            pltpu.VMEM((n_tm + 1, ext, nx), bf16),
            pltpu.VMEM((n_tm + 1, ext, nx), bf16),
            pltpu.VMEM((n_tm, spots * crows, LANES), f32),
            pltpu.VMEM((n_t, halves, nz * rows, LANES), f32),
            pltpu.VMEM((n_t, 2, halves, nz * rows, LANES), f32),
            pltpu.VMEM((8, LANES), f32),
            pltpu.VMEM((n_tm, spots, halves, wrows, LANES), f32),
            pltpu.VMEM((2, spots, halves, wrows, LANES), f32),
            pltpu.VMEM((n_tm, 8, LANES), f32),
            pltpu.VMEM((halves, n_tm, spots, crows, LANES), f32),
            pltpu.VMEM((halves, n_t, nz * rows, LANES), f32),
            pltpu.VMEM((n_tm, all_rows, nx), f32),
            pltpu.VMEM((n_tm, all_rows, nx), f32),
            pltpu.VMEM((2, all_rows, nx), f32),
            pltpu.VMEM((n_tm, all_rows, nx), f32),
            pltpu.VMEM((n_tm + 1, kept, nx), f32),
            pltpu.VMEM((n_tm + 1, kept, nx), f32),
            pltpu.VMEM((n_tm, halves, tail, LANES), f32),
            pltpu.VMEM((n_tm, halves, tail, LANES), f32),
            pltpu.SemaphoreType.DMA((count,)),
            pltpu.SemaphoreType.DMA((count,)),
            pltpu.SemaphoreType.DMA((2, spots)),
            pltpu.SemaphoreType.DMA((2, spots)),
            pltpu.SemaphoreType.DMA((n_tm,)),
            pltpu.SemaphoreType.DMA((n_tm,)),
            pltpu.SemaphoreType.DMA((halves, count)),
            pltpu.SemaphoreType.DMA((halves, count)),
            pltpu.SemaphoreType.DMA((n_tm + 1,)),
            pltpu.SemaphoreType.DMA((n_tm + 1,)),
            pltpu.SemaphoreType.DMA((n_tm, halves)),
            pltpu.SemaphoreType.DMA((n_tm, halves)),
        ],
        compiler_params=pltpu.CompilerParams(
            collective_id=0, has_side_effects=True, vmem_limit_bytes=63 * 1024 * 1024
        ),
    )(
        init_states.reshape(flat),
        forcing.reshape(flat),
        damp.reshape(flat),
        kappa_x[None],
        kappa_y[None],
        kappa_z[None],
        sea_tiles.reshape(1, -1),
        phases,
    )
    return out.reshape(init_states.shape)


def choose(init_states, forcing, damp, kappa_x, kappa_y, kappa_z, sea_tiles, phases):
    spots = lax.axis_size("space") // 2
    count = lax.axis_size("tm") * spots
    n_t, slabs, nx, rows, nz = init_states.shape
    ny = lax.axis_size("space") * rows
    per = max(count // n_t, 1)
    chunk = nz // per
    all_rows = spots * (chunk + 2 * HALO) * rows
    fits = (
        ITERS == 2
        and slabs == 1
        and lax.axis_size("space") % 2 == 0
        and lax.axis_size("tm") % 2 == 0
        and count % n_t == 0
        and nz == LANES
        and nx % LANES == 0
        and nz % per == 0
        and chunk * rows % 8 == 0
        and HALO * rows % 8 == 0
        and HALO <= chunk
        and chunk % 8 == 0
        and all_rows % 16 == 0
        and chunk + 2 * HALO <= nz
        and ny + 2 <= LANES
        and ny & (ny - 1) == 0
        and ny >= 16
        and sea_tiles.shape[1] == 1
        and all_rows + 2 * (chunk + HALO) <= 512
    )
    run = whole_period if fits else body
    return run(init_states, forcing, damp, kappa_x, kappa_y, kappa_z, sea_tiles, phases)


def solution(mesh):
    return jax.shard_map(
        choose,
        mesh=mesh,
        in_specs=(
            P(None, "tm", None, "space", None),
            P(None, None, "space", None),
            P(None, None, "space", None),
            P(),
            P(),
            P(),
            P(),
            P("tm"),
        ),
        out_specs=P(None, "tm", None, "space", None),
        check_vma=False,
    )
```

```python
import functools
import math

import jax
import jax.numpy as jnp
from jax import lax
from jax.experimental import pallas as pl
from jax.experimental.pallas import tpu as pltpu
from jax.sharding import PartitionSpec as P

STEPS = 2
ITERS = 2
TILE = 16
PHASES = 12


def shifted(array, axis, by):
    devices = lax.axis_size(axis)
    return lax.ppermute(array, axis, [(i, (i + by) % devices) for i in range(devices)])


def line_inverse(kappa):
    face = 0.5 * (kappa[1:] + kappa[:-1])
    zero = jnp.zeros((1,), kappa.dtype)
    left = jnp.concatenate([zero, face])
    right = jnp.concatenate([face, zero])
    identity = jnp.eye(kappa.shape[0], dtype=kappa.dtype)
    return lax.linalg.tridiagonal_solve(-left, 1.0 + left + right, -right, identity)


def solve_lines(field, inverse):
    return jnp.matmul(inverse, field, precision=lax.Precision.HIGHEST)


def solve_x(field, inverse):
    shape = field.shape
    flat = field.reshape(shape[0], shape[1], shape[2], shape[3] * shape[4])
    return solve_lines(flat, inverse).reshape(shape)


def vertical_mix(field, kappa_z):
    face = 0.5 * (kappa_z[1:] + kappa_z[:-1])
    flux = face * (field[..., 1:] - field[..., :-1])
    zeros = jnp.zeros(field.shape[:-1] + (1,), field.dtype)
    flux = jnp.concatenate([zeros, flux, zeros], axis=-1)
    return field + flux[..., 1:] - flux[..., :-1]


def compose(earlier, later):
    return (earlier[0] * later[0], later[0] * earlier[1] + later[1])


def column_pass(field, inverse_y):
    return lax.all_to_all(
        solve_lines(
            lax.all_to_all(field, "space", split_axis=2, concat_axis=3, tiled=True), inverse_y
        ),
        "space",
        split_axis=3,
        concat_axis=2,
        tiled=True,
    )


def body(init_states, forcing, damp, kappa_x, kappa_y, kappa_z, sea_tiles, phases):
    row_count = init_states.shape[3]
    inverse_x = line_inverse(kappa_x)
    inverse_y = line_inverse(kappa_y)
    tiles = sea_tiles.astype(jnp.float32)
    sea = jnp.repeat(jnp.repeat(tiles, TILE, axis=0), TILE, axis=1)
    sea_rows = lax.dynamic_slice_in_dim(sea, lax.axis_index("space") * row_count, row_count, 1)
    source = (forcing * sea_rows[None, :, :, None])[:, None]
    phase_float = phases.astype(jnp.float32)
    weight = 1.0 + 0.5 * jnp.cos(2.0 * math.pi * phase_float / PHASES)
    factors = jnp.exp(weight[None, :, None, None, None] * jnp.log(damp)[:, None])
    states = init_states
    for iteration in range(ITERS):
        field = states
        for step in range(STEPS):
            amplitude = jnp.cos(2.0 * math.pi * (phase_float * STEPS + step) / (PHASES * STEPS))[
                None, :, None, None, None
            ]
            if step % 2 == 0:
                field = column_pass(solve_x(field, inverse_x), inverse_y)
            else:
                field = solve_x(column_pass(field, inverse_y), inverse_x)
            field = vertical_mix(field, kappa_z) + amplitude * source
        offsets = field - factors * states
        own_factor = factors[:, 0]
        own_offset = offsets[:, 0]
        own = (own_factor, own_offset)
        ident = (jnp.ones_like(own_factor), jnp.zeros_like(own_offset))
        count = lax.axis_size("tm")
        here = lax.axis_index("tm")
        lower_part = ident
        upper_part = ident
        moving = jnp.stack([own_factor, own_offset])
        for turn in range(1, count):
            moving = shifted(moving, "tm", 1)
            piece = (moving[0], moving[1])
            anchor = (here - turn) % count
            before = anchor < here
            joined_low = compose(piece, lower_part)
            joined_high = compose(piece, upper_part)
            lower_part = (
                jnp.where(before, joined_low[0], lower_part[0]),
                jnp.where(before, joined_low[1], lower_part[1]),
            )
            upper_part = (
                jnp.where(before, upper_part[0], joined_high[0]),
                jnp.where(before, upper_part[1], joined_high[1]),
            )
        period = compose(compose(lower_part, own), upper_part)
        first = period[1] / (1.0 - period[0])
        start = lower_part[0] * first + lower_part[1]
        fresh = [start]
        states = jnp.stack(fresh, axis=1)
    return states


LANES = 128
HALO = 2 * ITERS
MESH = pl.DeviceIdType.MESH


def dot(a, b):
    return jnp.dot(a, b, precision=lax.Precision.HIGHEST, preferred_element_type=jnp.float32)


def parts(a):
    high = a.astype(jnp.bfloat16)
    return high, (a - high.astype(jnp.float32)).astype(jnp.bfloat16)


def dot3(a, b):
    once = functools.partial(jnp.dot, preferred_element_type=jnp.float32)
    return once(a[0], b[0]) + (once(a[0], b[1]) + once(a[1], b[0]))


def iota(shape, axis):
    return lax.broadcasted_iota(jnp.int32, shape, axis)


def faces(kappa_row, n):
    row, col = iota((n, n), 0), iota((n, n), 1)
    own = jnp.sum(jnp.where(row == col, kappa_row, 0.0), axis=1, keepdims=True)
    face = 0.5 * (own + kappa_row)
    below = jnp.where(col == row - 1, face, 0.0)
    above = jnp.where(col == row + 1, face, 0.0)
    return (
        jnp.sum(below, axis=1, keepdims=True),
        jnp.sum(above, axis=1, keepdims=True),
        below + above,
    )


def reduced_inverse(kappa_row, n):
    lower, upper, _ = faces(kappa_row, n)
    shape = (n, LANES)
    a = jnp.broadcast_to(-lower, shape)
    c = jnp.broadcast_to(-upper, shape)
    b = 1.0 - a - c
    blocks = [
        (iota(shape, 0) == iota(shape, 1) + LANES * j).astype(jnp.float32)
        for j in range(max(n // LANES, 1))
    ]
    s = 1
    while s < n:
        before = functools.partial(pltpu.roll, shift=s, axis=0)
        after = functools.partial(pltpu.roll, shift=n - s, axis=0)
        alpha = -a / before(b)
        gamma = -c / after(b)
        blocks = [d + alpha * before(d) + gamma * after(d) for d in blocks]
        b = b + alpha * before(c) + gamma * after(a)
        a, c = alpha * before(a), gamma * after(c)
        s *= 2
    inverse = 1.0 / b
    return [d * inverse for d in blocks]


def copied(pick, a):
    high, low = parts(a)
    once = functools.partial(jnp.dot, preferred_element_type=jnp.float32)
    return once(pick, high) + once(pick, low)


def spread(a, pick):
    high, low = parts(a)
    once = functools.partial(jnp.dot, preferred_element_type=jnp.float32)
    return once(high, pick) + once(low, pick)


def period_kernel(
    size, u_hbm, f_hbm, damp_hbm, kx_hbm, ky_hbm, kz_hbm, sea_hbm, phase_ref, out_ref,
    u_ref, f_ref, damp_ref, kx_ref, ky_ref, kz_ref, sea_ref, fetched, inverse_p,
    g_split, a_split, g_ref, a_ref, w_high, w_low, ends,
    ubuf, fbuf, pbuf, xbuf, dbuf, qbuf, obuf, state, factor, source, offset_ref,
    near_out, near_in, last_out, last_in,
    u_send, u_recv, f_send, f_recv, p_send, p_recv, o_send, o_recv,
    near_send, near_recv, last_send, last_recv,
):
    n_tm, n_sp, n_t, nx, rows, nz = size
    spots = n_sp // 2
    count = n_tm * spots
    per = count // n_t
    chunk = nz // per
    window = chunk + 2 * HALO
    halves = nx // LANES
    wrows = window * rows
    crows = chunk * rows
    all_rows = spots * wrows
    tail, kept = 2 * chunk, 2 * (chunk + HALO)
    ext = LANES * -(-(all_rows + kept) // LANES)
    ny = n_sp * rows

    here = lax.axis_index("tm")
    space = lax.axis_index("space")
    side, spot = space // spots, space % spots
    me = here * spots + spot
    across = {"tm": here, "space": (1 - side) * spots + spot}

    def window_start(k):
        return jnp.minimum(jnp.maximum(k * chunk - HALO, 0), nz - window)

    def window_rows(k):
        return pl.ds(pl.multiple_of(window_start(k) * rows, 8), wrows)

    def chunk_rows(k):
        return pl.ds(pl.multiple_of(k * crows, 8), crows)

    def device(index):
        return {"tm": index // spots, "space": side * spots + index % spots}

    pairs = (
        (u_hbm, u_ref),
        (f_hbm, f_ref),
        (damp_hbm, damp_ref),
        (kx_hbm, kx_ref),
        (ky_hbm, ky_ref),
        (kz_hbm, kz_ref),
        (sea_hbm, sea_ref),
    )
    fetches = [
        pltpu.make_async_copy(far, near, fetched.at[i]) for i, (far, near) in enumerate(pairs)
    ]
    for fetch in fetches:
        fetch.start()

    barrier = pltpu.get_barrier_semaphore()

    @pl.loop(1, count)
    def greet(offset):
        pl.semaphore_signal(
            barrier, inc=1, device_id=device((me + offset) % count), device_id_type=MESH
        )

    pl.semaphore_signal(barrier, inc=1, device_id=across, device_id_type=MESH)

    def turn(ref, buf, where):
        for t in range(n_t):
            for half in range(halves):
                for y in range(rows):
                    part = ref[t, pl.ds(half * LANES * rows + y, LANES, stride=rows), :]
                    buf[(t, *where, half, pl.ds(y, nz, stride=rows), slice(None))] = part.T

    pbuf[...] = jnp.full((8, LANES), phase_ref[0].astype(jnp.float32))

    my_t, my_k = me // per, me % per
    my_start = window_start(my_k)

    own_u = pltpu.make_async_copy(
        ubuf.at[my_t, :, window_rows(my_k), :], xbuf.at[me], u_recv.at[here]
    )
    own_f = [
        pltpu.make_async_copy(
            fbuf.at[my_t, which, :, window_rows(my_k), :],
            dbuf.at[which, spot],
            f_recv.at[which],
        )
        for which in range(2)
    ]
    own_p = pltpu.make_async_copy(pbuf, qbuf.at[here], p_recv)

    def send_u(offset):
        index = (me + offset) % count
        return pltpu.make_async_remote_copy(
            src_ref=ubuf.at[index // per, :, window_rows(index % per), :],
            dst_ref=xbuf.at[here * spots + spot],
            send_sem=u_send,
            recv_sem=u_recv.at[here],
            device_id=device(index),
            device_id_type=MESH,
        )

    def send_f(which, offset):
        index = here * spots + (spot + offset) % spots
        return pltpu.make_async_remote_copy(
            src_ref=fbuf.at[index // per, which, :, window_rows(index % per), :],
            dst_ref=dbuf.at[which, spot],
            send_sem=f_send,
            recv_sem=f_recv.at[which],
            device_id=device(index),
            device_id_type=MESH,
        )

    def send_p(offset):
        return pltpu.make_async_remote_copy(
            src_ref=pbuf,
            dst_ref=qbuf.at[here],
            send_sem=p_send,
            recv_sem=p_recv,
            device_id={"tm": (here + offset) % n_tm, "space": space},
            device_id_type=MESH,
        )

    def send_near(n):
        return pltpu.make_async_remote_copy(
            src_ref=near_out.at[n],
            dst_ref=near_in.at[n],
            send_sem=near_send,
            recv_sem=near_recv.at[n],
            device_id=across,
            device_id_type=MESH,
        )

    def send_last(n, half):
        return pltpu.make_async_remote_copy(
            src_ref=last_out.at[n, half],
            dst_ref=last_in.at[n, half],
            send_sem=last_send,
            recv_sem=last_recv.at[n, half],
            device_id=across,
            device_id_type=MESH,
        )

    def send_o(half, index):
        return pltpu.make_async_remote_copy(
            src_ref=obuf.at[half * count + index],
            dst_ref=out_ref.at[my_t, half, chunk_rows(my_k), :],
            send_sem=o_send,
            recv_sem=o_recv,
            device_id=device(index),
            device_id_type=MESH,
        )

    fetches[0].wait()
    turn(u_ref, ubuf, ())
    pl.semaphore_wait(barrier, count)

    @pl.loop(1, n_tm)
    def start_p(offset):
        send_p(offset).start()

    @pl.loop(1, count // 2 + 1)
    def start_u(offset):
        send_u(offset).start()

    own_p.start()
    own_u.start()
    fetches[1].wait()
    turn(f_ref, fbuf, (0,))

    @pl.loop(1, spots)
    def start_f(offset):
        send_f(0, offset).start()

    own_f[0].start()

    @pl.loop(count // 2 + 1, count)
    def start_u_rest(offset):
        send_u(offset).start()

    fetches[2].wait()
    turn(damp_ref, fbuf, (1,))

    for fetch in fetches[3:]:
        fetch.wait()

    for half, block in enumerate(reduced_inverse(kx_ref[...], nx)):
        a_ref[:, half * LANES : (half + 1) * LANES] = block
    a_once = a_ref[...]
    for i, part in enumerate(parts(a_once)):
        a_split[0, i] = part
    for i, part in enumerate(parts(dot(a_once, a_once))):
        a_split[1, i] = part

    inverse_y = reduced_inverse(ky_ref[...], ny)[0]
    row, col = iota((ny, LANES), 0), iota((ny, LANES), 1)
    edge, far_edge = ny // 2 - 1 + side, ny // 2 - side
    own_row, own_col = row // (ny // 2) == side, col // (ny // 2) == side
    inner_y = jnp.where(own_row & own_col, inverse_y, 0.0)
    twice_y = dot(inverse_y[:, :ny], inverse_y)
    inner_twice = dot(inner_y[:, :ny], inner_y)
    corner = jnp.sum(
        jnp.sum(
            jnp.where((row == far_edge) & (col == far_edge), inverse_y, 0.0), axis=1, keepdims=True
        ),
        axis=0,
        keepdims=True,
    )
    leave_once = jnp.sum(jnp.where(row == edge, inner_y, 0.0), axis=0, keepdims=True)
    leave_twice = jnp.sum(jnp.where(row == edge, inner_twice, 0.0), axis=0, keepdims=True)
    enter_line = (
        jnp.sum(jnp.where((row == far_edge) & own_col, inverse_y, 0.0), axis=0, keepdims=True)
        / corner
    )
    enter_once = (
        jnp.sum(jnp.where((col == far_edge) & own_row, inverse_y, 0.0), axis=1, keepdims=True)
        / corner
    )
    enter_twice = jnp.sum(inner_y * enter_line, axis=1, keepdims=True)
    below = iota((ny, LANES), 0)
    ext_y_once = jnp.concatenate(
        [
            inverse_y + jnp.where(col == ny, enter_once, 0.0),
            jnp.where(below == 0, leave_once, 0.0),
        ],
        axis=0,
    )
    ext_y_twice = jnp.concatenate(
        [
            twice_y
            + jnp.where(col == ny, enter_twice, 0.0)
            + jnp.where(col == ny + 1, enter_once, 0.0),
            jnp.where(below == 0, leave_once, jnp.where(below == 1, leave_twice, 0.0)),
        ],
        axis=0,
    )

    def line_of(q):
        own = side * (ny // 2) + (q // wrows) * rows + q % rows
        return jnp.where(q < all_rows, own, ny + q % 2)

    def level_of(q):
        own = my_start + (q % wrows) // rows
        p = (q - all_rows) // 2
        first = my_k * chunk
        ring = jnp.where(p < chunk + HALO // 2, first - HALO // 2 - chunk, first - HALO // 2) + p
        passed = jnp.where(p < chunk, first + p, ring)
        return jnp.where(q < all_rows, own, jnp.where(q < all_rows + kept, passed, -1))

    def mask(a, b):
        return jnp.where(a == b, 1.0, 0.0).astype(jnp.bfloat16)

    pick_y = mask(line_of(iota((ext, 2 * ny), 0)), iota((ext, 2 * ny), 1))
    pick_y_back = mask(line_of(iota((LANES, ext), 1)), iota((LANES, ext), 0))
    pick_z = mask(level_of(iota((ext, nz), 0)), iota((ext, nz), 1))
    pick_z_back = mask(level_of(iota((nz, ext), 1)), iota((nz, ext), 0))
    own_columns = iota((nz, ext), 1) < all_rows
    _, _, beside = faces(kz_ref[...], nz)
    identity = (iota((nz, nz), 0) == iota((nz, nz), 1)).astype(jnp.float32)
    vertical = beside + identity * (1.0 - jnp.sum(beside, axis=1, keepdims=True))
    for order, (ext_y, mixed) in enumerate(
        ((ext_y_once, vertical), (ext_y_twice, dot(vertical, vertical)))
    ):
        across_y = spread(copied(pick_y, ext_y), pick_y_back)
        levels = jnp.where(own_columns, spread(mixed, pick_z_back), pick_z_back.astype(jnp.float32))
        whole = across_y * copied(pick_z, levels)
        for i, part in enumerate(parts(whole)):
            g_split[order, i] = part
    g_ref[...] = whole
    inner = (my_k * chunk - my_start) * rows

    def inner_rows(r):
        return pl.ds(pl.multiple_of(r * wrows + inner, 8), crows)

    for i, part in enumerate(
        parts(jnp.concatenate([g_ref[inner_rows(r), :] for r in range(spots)], axis=0))
    ):
        g_split[2, i, : spots * crows, :] = part

    w_high[:, all_rows:, :] = jnp.zeros((n_tm + 1, ext - all_rows, nx), jnp.bfloat16)
    w_low[:, all_rows:, :] = jnp.zeros((n_tm + 1, ext - all_rows, nx), jnp.bfloat16)

    tile = (iota((nx // TILE, nx), 1) // TILE == iota((nx // TILE, nx), 0)).astype(jnp.float32)
    tiles = nx // TILE
    flags = jnp.where(
        iota((tiles, tiles), 0) == iota((tiles, tiles), 1), sea_ref[...].astype(jnp.float32), 0.0
    )
    sea = jnp.sum(jnp.sum(flags, axis=1, keepdims=True) * tile, axis=0, keepdims=True)

    def gathered(ref, where):
        return jnp.concatenate(
            [ref[where(half)].reshape(all_rows, LANES) for half in range(halves)], axis=1
        )

    def solve_x_lines(n, order, field):
        moved = dot3(parts(field), (a_split[order, 0], a_split[order, 1]))
        w_high[n, :all_rows, :], w_low[n, :all_rows, :] = parts(moved)

    def leaving(n, order, lines):
        padded = 16 * -(-lines // 16)
        block = slice(all_rows, all_rows + padded)
        found = dot3(
            (g_split[order, 0, block, :], g_split[order, 1, block, :]), (w_high[n], w_low[n])
        )
        return found[:lines]

    def joined(n, order):
        w_high[n, all_rows:, :], w_low[n, all_rows:, :] = parts(
            jnp.concatenate(
                [near_in[n], jnp.zeros((ext - all_rows - kept, nx), jnp.float32)], axis=0
            )
        )
        block = slice(0, all_rows)
        return dot3(
            (g_split[order, 0, block, :], g_split[order, 1, block, :]), (w_high[n], w_low[n])
        )

    def slab_of(n):
        return xbuf.at[pl.ds(n * spots, spots)]

    def arrive_u(turned):
        n = (here + n_tm - turned) % n_tm

        slot = slab_of(n)
        pltpu.make_async_copy(slot, slot, u_recv.at[n]).wait()
        solve_x_lines(n, 1, gathered(xbuf, lambda half: (pl.ds(n * spots, spots), half)))
        near_out[n] = leaving(n, 1, kept)
        send_near(n).start()

    pl.loop(1, n_tm // 2 + 1)(arrive_u)
    @pl.loop(1, spots)
    def start_damp(offset):
        send_f(1, offset).start()

    own_f[1].start()

    pltpu.make_async_copy(dbuf.at[0], dbuf.at[0], f_recv.at[0]).wait()

    source[1] = gathered(dbuf, lambda half: (0, slice(None), half)) * sea
    solve_x_lines(n_tm, 0, source[1])
    near_out[n_tm] = leaving(n_tm, 0, kept)
    send_near(n_tm).start()

    pl.loop(n_tm // 2 + 1, n_tm + 1)(arrive_u)

    pltpu.make_async_copy(qbuf, qbuf, p_recv).wait()
    pltpu.make_async_copy(dbuf.at[1], dbuf.at[1], f_recv.at[1]).wait()

    def wide(values):
        return jnp.concatenate([values[:1]] * halves, axis=1)

    log_damp = jnp.log(gathered(dbuf, lambda half: (1, slice(None), half)))
    product = None
    for n in range(n_tm):
        weight = 1.0 + 0.5 * jnp.cos(2.0 * math.pi * qbuf[n] / PHASES)
        one = jnp.exp(wide(weight) * log_damp)
        factor[n] = one
        product = one if product is None else one * product
    inverse_p[...] = 1.0 / (1.0 - product)

    def wait_near(n):
        pltpu.make_async_copy(near_in.at[n], near_in.at[n], near_recv.at[n]).wait()

    away = xbuf.at[pl.ds(0, count - 1)]
    pltpu.make_async_copy(away, away, u_send).wait()
    away = dbuf.at[:, pl.ds(0, spots - 1)]
    pltpu.make_async_copy(away, away, f_send).wait()
    away = qbuf.at[pl.ds(0, n_tm - 1)]
    pltpu.make_async_copy(away, away, p_send).wait()
    wait_near(n_tm)
    source[0] = joined(n_tm, 0)

    @pl.loop(0, n_tm)
    def make_offsets(n):
        phase = qbuf[n]
        first = jnp.cos(2.0 * math.pi * (phase * STEPS) / (PHASES * STEPS))
        second = jnp.cos(2.0 * math.pi * (phase * STEPS + 1) / (PHASES * STEPS))
        offset_ref[n] = wide(first) * source[0] + wide(second) * source[1]

    @pl.loop(1, n_tm + 1)
    def finish_first(turned):
        n = (here + n_tm - turned) % n_tm
        wait_near(n)
        field = gathered(xbuf, lambda half: (pl.ds(n * spots, spots), half))
        state[n] = joined(n, 1) + offset_ref[n] - factor[n] * field

    @pl.loop(0, spots)
    def solve_first(r):
        block = pl.ds(pl.multiple_of(r * wrows, 8), wrows)
        factors = [factor[n, block, :] for n in range(n_tm)]
        offsets = [state[n, block, :] for n in range(n_tm)]
        total = offsets[0]
        for n in range(1, n_tm):
            total = factors[n] * total + offsets[n]
        fresh = total * inverse_p[block, :]
        for n in range(n_tm):
            state[n, block, :] = fresh
            fresh = factors[n] * fresh + offsets[n]

    def lanes(half):
        return slice(half * LANES, (half + 1) * LANES)

    @pl.loop(0, n_tm)
    def leave_last(n):
        solve_x_lines(n, 1, state[n])
        found = leaving(n, 1, tail)
        for half in range(halves):
            last_out[n, half] = found[:, lanes(half)]
        send_last(n, 0).start()

    for half in range(1, halves):

        @pl.loop(0, n_tm)
        def start_last(n):
            send_last(n, half).start()

    pltpu.make_async_copy(near_in, near_in, near_send).wait()

    for half in range(halves):

        @pl.loop(0, n_tm)
        def finish_last(n):
            slot = last_in.at[n, half]
            pltpu.make_async_copy(slot, slot, last_recv.at[n, half]).wait()
            block = slice(all_rows, all_rows + tail)
            high, low = parts(last_in[n, half])
            w_high[n, block, lanes(half)] = high
            w_low[n, block, lanes(half)] = low
            upper = slice(0, spots * crows)
            ends[n] = dot3(
                (g_split[2, 0, upper, :], g_split[2, 1, upper, :]),
                (w_high[n, :, lanes(half)], w_low[n, :, lanes(half)]),
            )

        @pl.loop(1, spots + 1)
        def solve_last(turned):
            r = (spot + turned) % spots
            block = inner_rows(r)
            packed = pl.ds(pl.multiple_of(r * crows, 8), crows)
            factors = [factor[n, block, lanes(half)] for n in range(n_tm)]
            offsets = [
                ends[n, packed, :]
                + offset_ref[n, block, lanes(half)]
                - factors[n] * state[n, block, lanes(half)]
                for n in range(n_tm)
            ]
            total = offsets[0]
            for n in range(1, n_tm):
                total = factors[n] * total + offsets[n]
            fresh = total * inverse_p[block, lanes(half)]
            for n in range(n_tm):
                obuf[half * count + n * spots + r] = fresh
                fresh = factors[n] * fresh + offsets[n]
            for n in range(n_tm):

                @pl.when(n * spots + r != me)
                def _():
                    send_o(half, n * spots + r).start()

        pltpu.make_async_copy(
            obuf.at[half * count + me], out_ref.at[my_t, half, chunk_rows(my_k), :], o_recv
        ).start()

    pltpu.make_async_copy(last_in, last_in, last_send).wait()
    pltpu.make_async_copy(out_ref, out_ref, o_recv).wait()
    away = obuf.at[pl.ds(0, halves * (count - 1))]
    pltpu.make_async_copy(away, away, o_send).wait()


def turn_kernel(size, in_ref, out_ref, near_ref, turned_ref, in_sem, out_sem):
    n_t, halves, rows, nz = size
    blocks = [(t, half) for half in range(halves) for t in range(n_t)]

    def fetch(i):
        return pltpu.make_async_copy(in_ref.at[blocks[i]], near_ref.at[i], in_sem.at[i])

    def store(i):
        t, half = blocks[i]
        place = pl.ds(half * LANES * rows, LANES * rows)
        return pltpu.make_async_copy(turned_ref.at[i], out_ref.at[t, place, :], out_sem.at[i])

    for i in range(len(blocks)):
        fetch(i).start()
    for i in range(len(blocks)):
        fetch(i).wait()
        for y in range(rows):
            part = near_ref[i, pl.ds(y, nz, stride=rows), :]
            turned_ref[i, pl.ds(y, LANES, stride=rows), :] = part.T
        store(i).start()
    for i in range(len(blocks)):
        store(i).wait()


def whole_period(init_states, forcing, damp, kappa_x, kappa_y, kappa_z, sea_tiles, phases):
    n_tm, n_sp = lax.axis_size("tm"), lax.axis_size("space")
    n_t, _, nx, rows, nz = init_states.shape
    spots = n_sp // 2
    count = n_tm * spots
    chunk = nz // (count // n_t)
    window = chunk + 2 * HALO
    halves = nx // LANES
    wrows = window * rows
    crows = chunk * rows
    all_rows = spots * wrows
    tail, kept = 2 * chunk, 2 * (chunk + HALO)
    ext = LANES * -(-(all_rows + kept) // LANES)
    flat = (n_t, nx * rows, nz)
    f32 = jnp.float32
    bf16 = jnp.bfloat16
    landed = pl.pallas_call(
        functools.partial(period_kernel, (n_tm, n_sp, n_t, nx, rows, nz)),
        out_shape=jax.ShapeDtypeStruct((n_t, halves, nz * rows, LANES), f32),
        in_specs=[pl.BlockSpec(memory_space=pltpu.HBM)] * 7 + [pl.BlockSpec(memory_space=pltpu.SMEM)],
        out_specs=pl.BlockSpec(memory_space=pltpu.HBM),
        scratch_shapes=[
            pltpu.VMEM(flat, f32),
            pltpu.VMEM(flat, f32),
            pltpu.VMEM(flat, f32),
            pltpu.VMEM((1, nx), f32),
            pltpu.VMEM((1, kappa_y.shape[0]), f32),
            pltpu.VMEM((1, nz), f32),
            pltpu.VMEM((1, sea_tiles.shape[0]), jnp.int32),
            pltpu.SemaphoreType.DMA((7,)),
            pltpu.VMEM((all_rows, nx), f32),
            pltpu.VMEM((3, 2, ext, ext), bf16),
            pltpu.VMEM((2, 2, nx, nx), bf16),
            pltpu.VMEM((ext, ext), f32),
            pltpu.VMEM((nx, nx), f32),
            pltpu.VMEM((n_tm + 1, ext, nx), bf16),
            pltpu.VMEM((n_tm + 1, ext, nx), bf16),
            pltpu.VMEM((n_tm, spots * crows, LANES), f32),
            pltpu.VMEM((n_t, halves, nz * rows, LANES), f32),
            pltpu.VMEM((n_t, 2, halves, nz * rows, LANES), f32),
            pltpu.VMEM((8, LANES), f32),
            pltpu.VMEM((count, halves, wrows, LANES), f32),
            pltpu.VMEM((2, spots, halves, wrows, LANES), f32),
            pltpu.VMEM((n_tm, 8, LANES), f32),
            pltpu.VMEM((halves * count, crows, LANES), f32),
            pltpu.VMEM((n_tm, all_rows, nx), f32),
            pltpu.VMEM((n_tm, all_rows, nx), f32),
            pltpu.VMEM((2, all_rows, nx), f32),
            pltpu.VMEM((n_tm, all_rows, nx), f32),
            pltpu.VMEM((n_tm + 1, kept, nx), f32),
            pltpu.VMEM((n_tm + 1, kept, nx), f32),
            pltpu.VMEM((n_tm, halves, tail, LANES), f32),
            pltpu.VMEM((n_tm, halves, tail, LANES), f32),
            pltpu.SemaphoreType.DMA,
            pltpu.SemaphoreType.DMA((n_tm,)),
            pltpu.SemaphoreType.DMA,
            pltpu.SemaphoreType.DMA((2,)),
            pltpu.SemaphoreType.DMA,
            pltpu.SemaphoreType.DMA,
            pltpu.SemaphoreType.DMA,
            pltpu.SemaphoreType.DMA,
            pltpu.SemaphoreType.DMA,
            pltpu.SemaphoreType.DMA((n_tm + 1,)),
            pltpu.SemaphoreType.DMA,
            pltpu.SemaphoreType.DMA((n_tm, halves)),
        ],
        compiler_params=pltpu.CompilerParams(
            collective_id=0, has_side_effects=True, vmem_limit_bytes=63 * 1024 * 1024
        ),
    )(
        init_states.reshape(flat),
        forcing.reshape(flat),
        damp.reshape(flat),
        kappa_x[None],
        kappa_y[None],
        kappa_z[None],
        sea_tiles.reshape(1, -1),
        phases,
    )
    pieces = n_t * halves
    out = pl.pallas_call(
        functools.partial(turn_kernel, (n_t, halves, rows, nz)),
        out_shape=jax.ShapeDtypeStruct(flat, f32),
        in_specs=[pl.BlockSpec(memory_space=pl.ANY)],
        out_specs=pl.BlockSpec(memory_space=pl.ANY),
        scratch_shapes=[
            pltpu.VMEM((pieces, nz * rows, LANES), f32),
            pltpu.VMEM((pieces, LANES * rows, nz), f32),
            pltpu.SemaphoreType.DMA((pieces,)),
            pltpu.SemaphoreType.DMA((pieces,)),
        ],
    )(landed)
    return out.reshape(init_states.shape)


def choose(init_states, forcing, damp, kappa_x, kappa_y, kappa_z, sea_tiles, phases):
    spots = lax.axis_size("space") // 2
    count = lax.axis_size("tm") * spots
    n_t, slabs, nx, rows, nz = init_states.shape
    ny = lax.axis_size("space") * rows
    per = max(count // n_t, 1)
    chunk = nz // per
    all_rows = spots * (chunk + 2 * HALO) * rows
    fits = (
        ITERS == 2
        and slabs == 1
        and lax.axis_size("space") % 2 == 0
        and lax.axis_size("tm") % 2 == 0
        and count % n_t == 0
        and nz == LANES
        and nx % LANES == 0
        and nz % per == 0
        and chunk * rows % 8 == 0
        and HALO * rows % 8 == 0
        and HALO <= chunk
        and chunk % 8 == 0
        and all_rows % 16 == 0
        and chunk + 2 * HALO <= nz
        and ny + 2 <= LANES
        and ny & (ny - 1) == 0
        and ny >= 16
        and sea_tiles.shape[1] == 1
        and all_rows + 2 * (chunk + HALO) <= 512
    )
    run = whole_period if fits else body
    return run(init_states, forcing, damp, kappa_x, kappa_y, kappa_z, sea_tiles, phases)


def solution(mesh):
    return jax.shard_map(
        choose,
        mesh=mesh,
        in_specs=(
            P(None, "tm", None, "space", None),
            P(None, None, "space", None),
            P(None, None, "space", None),
            P(),
            P(),
            P(),
            P(),
            P("tm"),
        ),
        out_specs=P(None, "tm", None, "space", None),
        check_vma=False,
    )
```

```python
import functools
import math

import jax
import jax.numpy as jnp
from jax import lax
from jax.experimental import pallas as pl
from jax.experimental.pallas import tpu as pltpu
from jax.sharding import PartitionSpec as P

STEPS = 2
ITERS = 2
TILE = 16
PHASES = 12


def shifted(array, axis, by):
    devices = lax.axis_size(axis)
    return lax.ppermute(array, axis, [(i, (i + by) % devices) for i in range(devices)])


def line_inverse(kappa):
    face = 0.5 * (kappa[1:] + kappa[:-1])
    zero = jnp.zeros((1,), kappa.dtype)
    left = jnp.concatenate([zero, face])
    right = jnp.concatenate([face, zero])
    identity = jnp.eye(kappa.shape[0], dtype=kappa.dtype)
    return lax.linalg.tridiagonal_solve(-left, 1.0 + left + right, -right, identity)


def solve_lines(field, inverse):
    return jnp.matmul(inverse, field, precision=lax.Precision.HIGHEST)


def solve_x(field, inverse):
    shape = field.shape
    flat = field.reshape(shape[0], shape[1], shape[2], shape[3] * shape[4])
    return solve_lines(flat, inverse).reshape(shape)


def vertical_mix(field, kappa_z):
    face = 0.5 * (kappa_z[1:] + kappa_z[:-1])
    flux = face * (field[..., 1:] - field[..., :-1])
    zeros = jnp.zeros(field.shape[:-1] + (1,), field.dtype)
    flux = jnp.concatenate([zeros, flux, zeros], axis=-1)
    return field + flux[..., 1:] - flux[..., :-1]


def compose(earlier, later):
    return (earlier[0] * later[0], later[0] * earlier[1] + later[1])


def column_pass(field, inverse_y):
    return lax.all_to_all(
        solve_lines(
            lax.all_to_all(field, "space", split_axis=2, concat_axis=3, tiled=True), inverse_y
        ),
        "space",
        split_axis=3,
        concat_axis=2,
        tiled=True,
    )


def body(init_states, forcing, damp, kappa_x, kappa_y, kappa_z, sea_tiles, phases):
    row_count = init_states.shape[3]
    inverse_x = line_inverse(kappa_x)
    inverse_y = line_inverse(kappa_y)
    tiles = sea_tiles.astype(jnp.float32)
    sea = jnp.repeat(jnp.repeat(tiles, TILE, axis=0), TILE, axis=1)
    sea_rows = lax.dynamic_slice_in_dim(sea, lax.axis_index("space") * row_count, row_count, 1)
    source = (forcing * sea_rows[None, :, :, None])[:, None]
    phase_float = phases.astype(jnp.float32)
    weight = 1.0 + 0.5 * jnp.cos(2.0 * math.pi * phase_float / PHASES)
    factors = jnp.exp(weight[None, :, None, None, None] * jnp.log(damp)[:, None])
    states = init_states
    for iteration in range(ITERS):
        field = states
        for step in range(STEPS):
            amplitude = jnp.cos(2.0 * math.pi * (phase_float * STEPS + step) / (PHASES * STEPS))[
                None, :, None, None, None
            ]
            if step % 2 == 0:
                field = column_pass(solve_x(field, inverse_x), inverse_y)
            else:
                field = solve_x(column_pass(field, inverse_y), inverse_x)
            field = vertical_mix(field, kappa_z) + amplitude * source
        offsets = field - factors * states
        own_factor = factors[:, 0]
        own_offset = offsets[:, 0]
        own = (own_factor, own_offset)
        ident = (jnp.ones_like(own_factor), jnp.zeros_like(own_offset))
        count = lax.axis_size("tm")
        here = lax.axis_index("tm")
        lower_part = ident
        upper_part = ident
        moving = jnp.stack([own_factor, own_offset])
        for turn in range(1, count):
            moving = shifted(moving, "tm", 1)
            piece = (moving[0], moving[1])
            anchor = (here - turn) % count
            before = anchor < here
            joined_low = compose(piece, lower_part)
            joined_high = compose(piece, upper_part)
            lower_part = (
                jnp.where(before, joined_low[0], lower_part[0]),
                jnp.where(before, joined_low[1], lower_part[1]),
            )
            upper_part = (
                jnp.where(before, upper_part[0], joined_high[0]),
                jnp.where(before, upper_part[1], joined_high[1]),
            )
        period = compose(compose(lower_part, own), upper_part)
        first = period[1] / (1.0 - period[0])
        start = lower_part[0] * first + lower_part[1]
        fresh = [start]
        states = jnp.stack(fresh, axis=1)
    return states


LANES = 128
HALO = 2 * ITERS
GROUPS = 1
MESH = pl.DeviceIdType.MESH


def dot(a, b):
    return jnp.dot(a, b, precision=lax.Precision.HIGHEST, preferred_element_type=jnp.float32)


def parts(a):
    high = a.astype(jnp.bfloat16)
    return high, (a - high.astype(jnp.float32)).astype(jnp.bfloat16)


def dot3(a, b):
    once = functools.partial(jnp.dot, preferred_element_type=jnp.float32)
    lines = a[0].shape[0]
    both = once(jnp.concatenate(a, axis=0), b[0])
    return both[:lines] + (once(a[0], b[1]) + both[lines:])


def iota(shape, axis):
    return lax.broadcasted_iota(jnp.int32, shape, axis)


def faces(kappa_row, n):
    row, col = iota((n, n), 0), iota((n, n), 1)
    own = jnp.sum(jnp.where(row == col, kappa_row, 0.0), axis=1, keepdims=True)
    face = 0.5 * (own + kappa_row)
    below = jnp.where(col == row - 1, face, 0.0)
    above = jnp.where(col == row + 1, face, 0.0)
    return (
        jnp.sum(below, axis=1, keepdims=True),
        jnp.sum(above, axis=1, keepdims=True),
        below + above,
    )


def reduced_inverse(kappa_row, n):
    lower, upper, _ = faces(kappa_row, n)
    shape = (n, LANES)
    a = jnp.broadcast_to(-lower, shape)
    c = jnp.broadcast_to(-upper, shape)
    b = 1.0 - a - c
    blocks = [
        (iota(shape, 0) == iota(shape, 1) + LANES * j).astype(jnp.float32)
        for j in range(max(n // LANES, 1))
    ]
    s = 1
    while s < n:
        before = functools.partial(pltpu.roll, shift=s, axis=0)
        after = functools.partial(pltpu.roll, shift=n - s, axis=0)
        alpha = -a / before(b)
        gamma = -c / after(b)
        blocks = [d + alpha * before(d) + gamma * after(d) for d in blocks]
        b = b + alpha * before(c) + gamma * after(a)
        a, c = alpha * before(a), gamma * after(c)
        s *= 2
    inverse = 1.0 / b
    return [d * inverse for d in blocks]


def copied(pick, a):
    high, low = parts(a)
    once = functools.partial(jnp.dot, preferred_element_type=jnp.float32)
    return once(pick, high) + once(pick, low)


def spread(a, pick):
    high, low = parts(a)
    once = functools.partial(jnp.dot, preferred_element_type=jnp.float32)
    return once(high, pick) + once(low, pick)


def period_kernel(
    size, u_hbm, f_hbm, damp_hbm, kx_hbm, ky_hbm, kz_hbm, sea_hbm, phase_hbm, out_ref,
    u_ref, f_ref, damp_ref, kx_ref, ky_ref, kz_ref, sea_ref, phase_ref, fetched, inverse_p,
    g_split, a_split, g_ref, a_ref, w_high, w_low, mix, ends,
    ubuf, fbuf, pbuf, xbuf, dbuf, qbuf, obuf, state, factor, source, offset_ref,
    near_out, near_in, last_out, last_in,
    u_send, u_recv, f_send, f_recv, p_send, p_recv, o_send, o_recv,
    near_send, near_recv, last_send, last_recv,
):
    n_tm, n_sp, n_t, nx, rows, nz = size
    spots = n_sp // 2
    count = n_tm * spots
    per = count // n_t
    chunk = nz // per
    window = chunk + 2 * HALO
    halves = nx // LANES
    wrows = window * rows
    crows = chunk * rows
    all_rows = spots * wrows
    tail, kept = 2 * chunk, 2 * (chunk + HALO)
    ext = LANES * -(-(all_rows + kept) // LANES)
    ny = n_sp * rows
    pieces = [(half, group) for half in range(halves) for group in range(GROUPS)]
    prows = crows // GROUPS

    here = lax.axis_index("tm")
    space = lax.axis_index("space")
    side, spot = space // spots, space % spots
    me = here * spots + spot
    across = {"tm": here, "space": (1 - side) * spots + spot}

    def window_start(k):
        return jnp.minimum(jnp.maximum(k * chunk - HALO, 0), nz - window)

    def window_rows(k):
        return pl.ds(pl.multiple_of(window_start(k) * rows, 8), wrows)

    def chunk_rows(k):
        return pl.ds(pl.multiple_of(k * crows, 8), crows)

    def device(index):
        return {"tm": index // spots, "space": side * spots + index % spots}

    pairs = (
        (u_hbm, u_ref),
        (f_hbm, f_ref),
        (damp_hbm, damp_ref),
        (kx_hbm, kx_ref),
        (ky_hbm, ky_ref),
        (kz_hbm, kz_ref),
        (sea_hbm, sea_ref),
        (phase_hbm, phase_ref),
    )
    fetches = [
        pltpu.make_async_copy(far, near, fetched.at[i]) for i, (far, near) in enumerate(pairs)
    ]
    for fetch in fetches:
        fetch.start()

    barrier = pltpu.get_barrier_semaphore()

    @pl.loop(1, count)
    def greet(offset):
        pl.semaphore_signal(
            barrier, inc=1, device_id=device((me + offset) % count), device_id_type=MESH
        )

    pl.semaphore_signal(barrier, inc=1, device_id=across, device_id_type=MESH)

    def turn(ref, buf, where):
        for t in range(n_t):
            for half in range(halves):
                for y in range(rows):
                    part = ref[t, pl.ds(half * LANES * rows + y, LANES, stride=rows), :]
                    buf[(t, *where, half, pl.ds(y, nz, stride=rows), slice(None))] = part.T

    fetches[7].wait()
    pbuf[...] = jnp.broadcast_to(phase_ref[...].astype(jnp.float32), (8, LANES))

    my_t, my_k = me // per, me % per
    my_start = window_start(my_k)

    own_u = pltpu.make_async_copy(
        ubuf.at[my_t, :, window_rows(my_k), :], xbuf.at[me], u_recv.at[here]
    )
    own_f = [
        pltpu.make_async_copy(
            fbuf.at[my_t, which, :, window_rows(my_k), :],
            dbuf.at[which, spot],
            f_recv.at[which],
        )
        for which in range(2)
    ]
    own_p = pltpu.make_async_copy(pbuf, qbuf.at[here], p_recv)

    def send_u(offset):
        index = (here ^ (offset // spots)) * spots + (spot ^ (offset % spots))
        return pltpu.make_async_remote_copy(
            src_ref=ubuf.at[index // per, :, window_rows(index % per), :],
            dst_ref=xbuf.at[here * spots + spot],
            send_sem=u_send,
            recv_sem=u_recv.at[here],
            device_id=device(index),
            device_id_type=MESH,
        )

    def send_f(which, offset):
        index = here * spots + (spot + offset) % spots
        return pltpu.make_async_remote_copy(
            src_ref=fbuf.at[index // per, which, :, window_rows(index % per), :],
            dst_ref=dbuf.at[which, spot],
            send_sem=f_send,
            recv_sem=f_recv.at[which],
            device_id=device(index),
            device_id_type=MESH,
        )

    def send_p(offset):
        return pltpu.make_async_remote_copy(
            src_ref=pbuf,
            dst_ref=qbuf.at[here],
            send_sem=p_send,
            recv_sem=p_recv,
            device_id={"tm": (here + offset) % n_tm, "space": space},
            device_id_type=MESH,
        )

    def send_near(n):
        return pltpu.make_async_remote_copy(
            src_ref=near_out.at[n],
            dst_ref=near_in.at[n],
            send_sem=near_send,
            recv_sem=near_recv.at[n],
            device_id=across,
            device_id_type=MESH,
        )

    def send_last(n, piece):
        return pltpu.make_async_remote_copy(
            src_ref=last_out.at[piece, n],
            dst_ref=last_in.at[piece, n],
            send_sem=last_send,
            recv_sem=last_recv.at[piece],
            device_id=across,
            device_id_type=MESH,
        )

    def landing(piece):
        half, group = pieces[piece]
        place = pl.ds(pl.multiple_of(my_k * crows + group * prows, 8), prows)
        return out_ref.at[my_t, half, place, :]

    def send_o(piece, index):
        return pltpu.make_async_remote_copy(
            src_ref=obuf.at[piece * count + index],
            dst_ref=landing(piece),
            send_sem=o_send,
            recv_sem=o_recv,
            device_id=device(index),
            device_id_type=MESH,
        )

    fetches[0].wait()
    turn(u_ref, ubuf, ())
    pl.semaphore_wait(barrier, count)

    @pl.loop(1, n_tm)
    def start_p(offset):
        send_p(offset).start()

    for offset in (11, 10, 9, 8, 15, 14, 13, 12):
        send_u(offset).start()

    own_p.start()
    own_u.start()
    fetches[1].wait()
    turn(f_ref, fbuf, (0,))

    @pl.loop(1, spots)
    def start_f(offset):
        send_f(0, offset).start()

    own_f[0].start()

    for offset in (7, 6, 5, 4, 3, 2, 1):
        send_u(offset).start()

    fetches[2].wait()
    turn(damp_ref, fbuf, (1,))

    for fetch in fetches[3:7]:
        fetch.wait()

    for half, block in enumerate(reduced_inverse(kx_ref[...], nx)):
        a_ref[:, half * LANES : (half + 1) * LANES] = block
    a_once = a_ref[...]
    for i, part in enumerate(parts(a_once)):
        a_split[0, i] = part
    for i, part in enumerate(parts(dot(a_once, a_once))):
        a_split[1, i] = part

    inverse_y = reduced_inverse(ky_ref[...], ny)[0]
    row, col = iota((ny, LANES), 0), iota((ny, LANES), 1)
    edge, far_edge = ny // 2 - 1 + side, ny // 2 - side
    own_row, own_col = row // (ny // 2) == side, col // (ny // 2) == side
    inner_y = jnp.where(own_row & own_col, inverse_y, 0.0)
    twice_y = dot(inverse_y[:, :ny], inverse_y)
    inner_twice = dot(inner_y[:, :ny], inner_y)
    corner = jnp.sum(
        jnp.sum(
            jnp.where((row == far_edge) & (col == far_edge), inverse_y, 0.0), axis=1, keepdims=True
        ),
        axis=0,
        keepdims=True,
    )
    leave_once = jnp.sum(jnp.where(row == edge, inner_y, 0.0), axis=0, keepdims=True)
    leave_twice = jnp.sum(jnp.where(row == edge, inner_twice, 0.0), axis=0, keepdims=True)
    enter_line = (
        jnp.sum(jnp.where((row == far_edge) & own_col, inverse_y, 0.0), axis=0, keepdims=True)
        / corner
    )
    enter_once = (
        jnp.sum(jnp.where((col == far_edge) & own_row, inverse_y, 0.0), axis=1, keepdims=True)
        / corner
    )
    enter_twice = jnp.sum(inner_y * enter_line, axis=1, keepdims=True)
    below = iota((ny, LANES), 0)
    ext_y_once = jnp.concatenate(
        [
            inverse_y + jnp.where(col == ny, enter_once, 0.0),
            jnp.where(below == 0, leave_once, 0.0),
        ],
        axis=0,
    )
    ext_y_twice = jnp.concatenate(
        [
            twice_y
            + jnp.where(col == ny, enter_twice, 0.0)
            + jnp.where(col == ny + 1, enter_once, 0.0),
            jnp.where(below == 0, leave_once, jnp.where(below == 1, leave_twice, 0.0)),
        ],
        axis=0,
    )

    def line_of(q):
        own = side * (ny // 2) + (q // wrows) * rows + q % rows
        return jnp.where(q < all_rows, own, ny + q % 2)

    def level_of(q):
        own = my_start + (q % wrows) // rows
        p = (q - all_rows) // 2
        first = my_k * chunk
        ring = jnp.where(p < chunk + HALO // 2, first - HALO // 2 - chunk, first - HALO // 2) + p
        passed = jnp.where(p < chunk, first + p, ring)
        return jnp.where(q < all_rows, own, jnp.where(q < all_rows + kept, passed, -1))

    def mask(a, b):
        return jnp.where(a == b, 1.0, 0.0).astype(jnp.bfloat16)

    pick_y = mask(line_of(iota((ext, 2 * ny), 0)), iota((ext, 2 * ny), 1))
    pick_y_back = mask(line_of(iota((LANES, ext), 1)), iota((LANES, ext), 0))
    pick_z = mask(level_of(iota((ext, nz), 0)), iota((ext, nz), 1))
    pick_z_back = mask(level_of(iota((nz, ext), 1)), iota((nz, ext), 0))
    own_columns = iota((nz, ext), 1) < all_rows
    _, _, beside = faces(kz_ref[...], nz)
    identity = (iota((nz, nz), 0) == iota((nz, nz), 1)).astype(jnp.float32)
    vertical = beside + identity * (1.0 - jnp.sum(beside, axis=1, keepdims=True))
    for order, (ext_y, mixed) in enumerate(
        ((ext_y_once, vertical), (ext_y_twice, dot(vertical, vertical)))
    ):
        across_y = spread(copied(pick_y, ext_y), pick_y_back)
        levels = jnp.where(own_columns, spread(mixed, pick_z_back), pick_z_back.astype(jnp.float32))
        whole = across_y * copied(pick_z, levels)
        for i, part in enumerate(parts(whole)):
            g_split[order, i] = part
    g_ref[...] = whole
    inner = (my_k * chunk - my_start) * rows

    def inner_rows(r):
        return pl.ds(pl.multiple_of(r * wrows + inner, 8), crows)

    inner_g = jnp.concatenate([g_ref[inner_rows(r), :] for r in range(spots)], axis=0)
    inner_g = jnp.where(iota((spots * crows, ext), 1) < all_rows, inner_g, 0.0)
    for i, part in enumerate(parts(inner_g)):
        g_split[2, i, : spots * crows, :] = part
    q = iota((spots * prows, LANES), 0)
    picked = side * (ny // 2) + (q // prows) * rows + q % rows
    picked = jnp.where(picked == iota((spots * prows, LANES), 1), 1.0, 0.0)[:, :ny]
    enters = [dot(picked, jnp.broadcast_to(c, (ny, LANES))) for c in (enter_twice, enter_once)]
    mix[0] = jnp.where(q % 2 == 0, enters[0], enters[1])
    mix[1] = jnp.where(q % 2 == 0, enters[1], enters[0])

    w_high[:, all_rows:, :] = jnp.zeros((n_tm + 1, ext - all_rows, nx), jnp.bfloat16)
    w_low[:, all_rows:, :] = jnp.zeros((n_tm + 1, ext - all_rows, nx), jnp.bfloat16)

    tile = (iota((nx // TILE, nx), 1) // TILE == iota((nx // TILE, nx), 0)).astype(jnp.float32)
    tiles = nx // TILE
    flags = jnp.where(
        iota((tiles, tiles), 0) == iota((tiles, tiles), 1), sea_ref[...].astype(jnp.float32), 0.0
    )
    sea = jnp.sum(jnp.sum(flags, axis=1, keepdims=True) * tile, axis=0, keepdims=True)

    def gathered(ref, where):
        return jnp.concatenate(
            [ref[where(half)].reshape(all_rows, LANES) for half in range(halves)], axis=1
        )

    def solve_x_lines(n, order, field):
        moved = dot3(parts(field), (a_split[order, 0], a_split[order, 1]))
        w_high[n, :all_rows, :], w_low[n, :all_rows, :] = parts(moved)

    def leaving(n, order, lines):
        padded = 16 * -(-lines // 16)
        block = slice(all_rows, all_rows + padded)
        found = dot3(
            (g_split[order, 0, block, :], g_split[order, 1, block, :]), (w_high[n], w_low[n])
        )
        return found[:lines]

    def joined(n, order):
        w_high[n, all_rows:, :], w_low[n, all_rows:, :] = parts(
            jnp.concatenate(
                [near_in[n], jnp.zeros((ext - all_rows - kept, nx), jnp.float32)], axis=0
            )
        )
        block = slice(0, all_rows)
        return dot3(
            (g_split[order, 0, block, :], g_split[order, 1, block, :]), (w_high[n], w_low[n])
        )

    def slab_of(n):
        return xbuf.at[pl.ds(n * spots, spots)]

    def arrive_u(turned):
        n = here ^ ((turned + 1) % n_tm)

        slot = slab_of(n)
        pltpu.make_async_copy(slot, slot, u_recv.at[n]).wait()
        solve_x_lines(n, 1, gathered(xbuf, lambda half: (pl.ds(n * spots, spots), half)))
        near_out[n] = leaving(n, 1, kept)
        send_near(n).start()

    pl.loop(1, n_tm // 2 + 1)(arrive_u)
    @pl.loop(1, spots)
    def start_damp(offset):
        send_f(1, offset).start()

    own_f[1].start()

    pltpu.make_async_copy(dbuf.at[0], dbuf.at[0], f_recv.at[0]).wait()

    source[1] = gathered(dbuf, lambda half: (0, slice(None), half)) * sea
    solve_x_lines(n_tm, 0, source[1])
    near_out[n_tm] = leaving(n_tm, 0, kept)
    send_near(n_tm).start()

    pl.loop(n_tm // 2 + 1, n_tm + 1)(arrive_u)

    pltpu.make_async_copy(qbuf, qbuf, p_recv).wait()
    pltpu.make_async_copy(dbuf.at[1], dbuf.at[1], f_recv.at[1]).wait()

    def wide(values):
        return jnp.concatenate([values[:1]] * halves, axis=1)

    log_damp = jnp.log(gathered(dbuf, lambda half: (1, slice(None), half)))
    product = None
    for n in range(n_tm):
        weight = 1.0 + 0.5 * jnp.cos(2.0 * math.pi * qbuf[n] / PHASES)
        one = jnp.exp(wide(weight) * log_damp)
        factor[n] = one
        product = one if product is None else one * product
    inverse_p[...] = 1.0 / (1.0 - product)

    def wait_near(n):
        pltpu.make_async_copy(near_in.at[n], near_in.at[n], near_recv.at[n]).wait()

    away = xbuf.at[pl.ds(0, count - 1)]
    pltpu.make_async_copy(away, away, u_send).wait()
    away = dbuf.at[:, pl.ds(0, spots - 1)]
    pltpu.make_async_copy(away, away, f_send).wait()
    away = qbuf.at[pl.ds(0, n_tm - 1)]
    pltpu.make_async_copy(away, away, p_send).wait()
    wait_near(n_tm)
    source[0] = joined(n_tm, 0)

    @pl.loop(0, n_tm)
    def make_offsets(n):
        phase = qbuf[n]
        first = jnp.cos(2.0 * math.pi * (phase * STEPS) / (PHASES * STEPS))
        second = jnp.cos(2.0 * math.pi * (phase * STEPS + 1) / (PHASES * STEPS))
        offset_ref[n] = wide(first) * source[0] + wide(second) * source[1]

    @pl.loop(1, n_tm + 1)
    def finish_first(turned):
        n = here ^ ((turned + 1) % n_tm)
        wait_near(n)
        field = gathered(xbuf, lambda half: (pl.ds(n * spots, spots), half))
        state[n] = joined(n, 1) + offset_ref[n] - factor[n] * field

    @pl.loop(0, spots)
    def solve_first(r):
        block = pl.ds(pl.multiple_of(r * wrows, 8), wrows)
        factors = [factor[n, block, :] for n in range(n_tm)]
        offsets = [state[n, block, :] for n in range(n_tm)]
        total = offsets[0]
        for n in range(1, n_tm):
            total = factors[n] * total + offsets[n]
        fresh = total * inverse_p[block, :]
        for n in range(n_tm):
            state[n, block, :] = fresh
            fresh = factors[n] * fresh + offsets[n]

    def lanes(half):
        return slice(half * LANES, (half + 1) * LANES)

    first_pieces = 1

    for n in range(n_tm):
        solve_x_lines(n, 1, state[n])
    for n in range(n_tm):
        found = leaving(n, 1, tail)
        for piece, (half, group) in enumerate(pieces):
            last_out[piece, n] = found[group * prows : (group + 1) * prows, lanes(half)]
        for piece in range(first_pieces):
            send_last(n, piece).start()

    for piece in range(first_pieces, len(pieces)):

        @pl.loop(0, n_tm)
        def start_last(n):
            send_last(n, piece).start()

    pltpu.make_async_copy(near_in, near_in, near_send).wait()

    @pl.loop(0, n_tm)
    def own_last(n):
        upper = slice(0, spots * crows)
        own = dot3(
            (g_split[2, 0, upper, :], g_split[2, 1, upper, :]), (w_high[n], w_low[n])
        )
        for r in range(spots):
            packed = slice(r * crows, (r + 1) * crows)
            block = inner_rows(r)
            ends[n, packed, :] = (
                own[packed] + offset_ref[n, block, :] - factor[n, block, :] * state[n, block, :]
            )

    even = iota((prows, LANES), 0) % 2 == 0

    def swapped(a):
        return jnp.where(even, pltpu.roll(a, prows - 1, 0), pltpu.roll(a, 1, 0))

    for piece, (half, group) in enumerate(pieces):
        slot = last_in.at[piece]
        pltpu.make_async_copy(slot, slot, last_recv.at[piece]).wait()

        def solve_last(turned):
            r = (spot + turned) % spots
            block = pl.ds(pl.multiple_of(r * wrows + inner + group * prows, 8), prows)
            packed = pl.ds(pl.multiple_of(r * crows + group * prows, 8), prows)
            mine = pl.ds(pl.multiple_of(r * prows, 8), prows)
            factors = [factor[n, block, lanes(half)] for n in range(n_tm)]
            offsets = []
            for n in range(n_tm):
                entering = last_in[piece, n]
                offsets.append(
                    ends[n, packed, lanes(half)]
                    + mix[0, mine, :] * entering
                    + mix[1, mine, :] * swapped(entering)
                )
            total = offsets[0]
            for n in range(1, n_tm):
                total = factors[n] * total + offsets[n]
            fresh = total * inverse_p[block, lanes(half)]
            for n in range(n_tm):
                obuf[piece * count + n * spots + r] = fresh
                fresh = factors[n] * fresh + offsets[n]
            for n in range(n_tm):

                @pl.when(n * spots + r != me)
                def _():
                    send_o(piece, n * spots + r).start()

        for turned in range(1, spots + 1):
            solve_last(turned)
        pltpu.make_async_copy(obuf.at[piece * count + me], landing(piece), o_recv).start()

    pltpu.make_async_copy(last_in, last_in, last_send).wait()
    pltpu.make_async_copy(out_ref, out_ref, o_recv).wait()
    away = obuf.at[pl.ds(0, len(pieces) * (count - 1))]
    pltpu.make_async_copy(away, away, o_send).wait()


def turn_kernel(size, in_ref, out_ref, near_ref, turned_ref, in_sem, out_sem):
    n_t, halves, rows, nz = size
    blocks = [(t, half) for half in range(halves) for t in range(n_t)]

    def fetch(i):
        return pltpu.make_async_copy(in_ref.at[blocks[i]], near_ref.at[i], in_sem.at[i])

    def store(i):
        t, half = blocks[i]
        place = pl.ds(half * LANES * rows, LANES * rows)
        return pltpu.make_async_copy(turned_ref.at[i], out_ref.at[t, place, :], out_sem.at[i])

    for i in range(len(blocks)):
        fetch(i).start()
    for i in range(len(blocks)):
        fetch(i).wait()
        for y in range(rows):
            part = near_ref[i, pl.ds(y, nz, stride=rows), :]
            turned_ref[i, pl.ds(y, LANES, stride=rows), :] = part.T
        store(i).start()
    for i in range(len(blocks)):
        store(i).wait()


def whole_period(init_states, forcing, damp, kappa_x, kappa_y, kappa_z, sea_tiles, phases):
    n_tm, n_sp = lax.axis_size("tm"), lax.axis_size("space")
    n_t, _, nx, rows, nz = init_states.shape
    spots = n_sp // 2
    count = n_tm * spots
    chunk = nz // (count // n_t)
    window = chunk + 2 * HALO
    halves = nx // LANES
    wrows = window * rows
    crows = chunk * rows
    all_rows = spots * wrows
    kept = 2 * (chunk + HALO)
    prows = crows // GROUPS
    ext = LANES * -(-(all_rows + kept) // LANES)
    flat = (n_t, nx * rows, nz)
    f32 = jnp.float32
    bf16 = jnp.bfloat16
    landed = pl.pallas_call(
        functools.partial(period_kernel, (n_tm, n_sp, n_t, nx, rows, nz)),
        out_shape=jax.ShapeDtypeStruct((n_t, halves, nz * rows, LANES), f32),
        in_specs=[pl.BlockSpec(memory_space=pltpu.HBM)] * 8,
        out_specs=pl.BlockSpec(memory_space=pltpu.HBM),
        scratch_shapes=[
            pltpu.VMEM(flat, f32),
            pltpu.VMEM(flat, f32),
            pltpu.VMEM(flat, f32),
            pltpu.VMEM((1, nx), f32),
            pltpu.VMEM((1, kappa_y.shape[0]), f32),
            pltpu.VMEM((1, nz), f32),
            pltpu.VMEM((1, sea_tiles.shape[0]), jnp.int32),
            pltpu.VMEM((1, 1), jnp.int32),
            pltpu.SemaphoreType.DMA((8,)),
            pltpu.VMEM((all_rows, nx), f32),
            pltpu.VMEM((3, 2, ext, ext), bf16),
            pltpu.VMEM((2, 2, nx, nx), bf16),
            pltpu.VMEM((ext, ext), f32),
            pltpu.VMEM((nx, nx), f32),
            pltpu.VMEM((n_tm + 1, ext, nx), bf16),
            pltpu.VMEM((n_tm + 1, ext, nx), bf16),
            pltpu.VMEM((2, spots * prows, LANES), f32),
            pltpu.VMEM((n_tm, spots * crows, nx), f32),
            pltpu.VMEM((n_t, halves, nz * rows, LANES), f32),
            pltpu.VMEM((n_t, 2, halves, nz * rows, LANES), f32),
            pltpu.VMEM((8, LANES), f32),
            pltpu.VMEM((count, halves, wrows, LANES), f32),
            pltpu.VMEM((2, spots, halves, wrows, LANES), f32),
            pltpu.VMEM((n_tm, 8, LANES), f32),
            pltpu.VMEM((halves * GROUPS * count, prows, LANES), f32),
            pltpu.VMEM((n_tm, all_rows, nx), f32),
            pltpu.VMEM((n_tm, all_rows, nx), f32),
            pltpu.VMEM((2, all_rows, nx), f32),
            pltpu.VMEM((n_tm, all_rows, nx), f32),
            pltpu.VMEM((n_tm + 1, kept, nx), f32),
            pltpu.VMEM((n_tm + 1, kept, nx), f32),
            pltpu.VMEM((halves * GROUPS, n_tm, prows, LANES), f32),
            pltpu.VMEM((halves * GROUPS, n_tm, prows, LANES), f32),
            pltpu.SemaphoreType.DMA,
            pltpu.SemaphoreType.DMA((n_tm,)),
            pltpu.SemaphoreType.DMA,
            pltpu.SemaphoreType.DMA((2,)),
            pltpu.SemaphoreType.DMA,
            pltpu.SemaphoreType.DMA,
            pltpu.SemaphoreType.DMA,
            pltpu.SemaphoreType.DMA,
            pltpu.SemaphoreType.DMA,
            pltpu.SemaphoreType.DMA((n_tm + 1,)),
            pltpu.SemaphoreType.DMA,
            pltpu.SemaphoreType.DMA((halves * GROUPS,)),
        ],
        compiler_params=pltpu.CompilerParams(
            collective_id=0, has_side_effects=True, vmem_limit_bytes=63 * 1024 * 1024
        ),
    )(
        init_states.reshape(flat),
        forcing.reshape(flat),
        damp.reshape(flat),
        kappa_x[None],
        kappa_y[None],
        kappa_z[None],
        sea_tiles.reshape(1, -1),
        phases.reshape(1, 1),
    )
    pieces = n_t * halves
    out = pl.pallas_call(
        functools.partial(turn_kernel, (n_t, halves, rows, nz)),
        out_shape=jax.ShapeDtypeStruct(flat, f32),
        in_specs=[pl.BlockSpec(memory_space=pl.ANY)],
        out_specs=pl.BlockSpec(memory_space=pl.ANY),
        scratch_shapes=[
            pltpu.VMEM((pieces, nz * rows, LANES), f32),
            pltpu.VMEM((pieces, LANES * rows, nz), f32),
            pltpu.SemaphoreType.DMA((pieces,)),
            pltpu.SemaphoreType.DMA((pieces,)),
        ],
    )(landed)
    return out.reshape(init_states.shape)


def choose(init_states, forcing, damp, kappa_x, kappa_y, kappa_z, sea_tiles, phases):
    spots = lax.axis_size("space") // 2
    count = lax.axis_size("tm") * spots
    n_t, slabs, nx, rows, nz = init_states.shape
    ny = lax.axis_size("space") * rows
    per = max(count // n_t, 1)
    chunk = nz // per
    all_rows = spots * (chunk + 2 * HALO) * rows
    fits = (
        ITERS == 2
        and slabs == 1
        and lax.axis_size("space") % 2 == 0
        and lax.axis_size("tm") % 2 == 0
        and count % n_t == 0
        and nz == LANES
        and nx % LANES == 0
        and nz % per == 0
        and rows == 2
        and chunk * rows % (8 * GROUPS) == 0
        and HALO * rows % 8 == 0
        and HALO <= chunk
        and chunk % 8 == 0
        and all_rows % 16 == 0
        and chunk + 2 * HALO <= nz
        and ny + 2 <= LANES
        and ny & (ny - 1) == 0
        and ny >= 16
        and sea_tiles.shape[1] == 1
        and all_rows + 2 * (chunk + HALO) <= 512
    )
    run = whole_period if fits else body
    return run(init_states, forcing, damp, kappa_x, kappa_y, kappa_z, sea_tiles, phases)


def solution(mesh):
    return jax.shard_map(
        choose,
        mesh=mesh,
        in_specs=(
            P(None, "tm", None, "space", None),
            P(None, None, "space", None),
            P(None, None, "space", None),
            P(),
            P(),
            P(),
            P(),
            P("tm"),
        ),
        out_specs=P(None, "tm", None, "space", None),
        check_vma=False,
    )
```

```python
import functools
import math

import jax
import jax.numpy as jnp
from jax import lax
from jax.experimental import pallas as pl
from jax.experimental.pallas import tpu as pltpu
from jax.sharding import PartitionSpec as P

STEPS = 2
ITERS = 2
TILE = 16
PHASES = 12


def shifted(array, axis, by):
    devices = lax.axis_size(axis)
    return lax.ppermute(array, axis, [(i, (i + by) % devices) for i in range(devices)])


def line_inverse(kappa):
    face = 0.5 * (kappa[1:] + kappa[:-1])
    zero = jnp.zeros((1,), kappa.dtype)
    left = jnp.concatenate([zero, face])
    right = jnp.concatenate([face, zero])
    identity = jnp.eye(kappa.shape[0], dtype=kappa.dtype)
    return lax.linalg.tridiagonal_solve(-left, 1.0 + left + right, -right, identity)


def solve_lines(field, inverse):
    return jnp.matmul(inverse, field, precision=lax.Precision.HIGHEST)


def solve_x(field, inverse):
    shape = field.shape
    flat = field.reshape(shape[0], shape[1], shape[2], shape[3] * shape[4])
    return solve_lines(flat, inverse).reshape(shape)


def vertical_mix(field, kappa_z):
    face = 0.5 * (kappa_z[1:] + kappa_z[:-1])
    flux = face * (field[..., 1:] - field[..., :-1])
    zeros = jnp.zeros(field.shape[:-1] + (1,), field.dtype)
    flux = jnp.concatenate([zeros, flux, zeros], axis=-1)
    return field + flux[..., 1:] - flux[..., :-1]


def compose(earlier, later):
    return (earlier[0] * later[0], later[0] * earlier[1] + later[1])


def column_pass(field, inverse_y):
    return lax.all_to_all(
        solve_lines(
            lax.all_to_all(field, "space", split_axis=2, concat_axis=3, tiled=True), inverse_y
        ),
        "space",
        split_axis=3,
        concat_axis=2,
        tiled=True,
    )


def body(init_states, forcing, damp, kappa_x, kappa_y, kappa_z, sea_tiles, phases):
    row_count = init_states.shape[3]
    inverse_x = line_inverse(kappa_x)
    inverse_y = line_inverse(kappa_y)
    tiles = sea_tiles.astype(jnp.float32)
    sea = jnp.repeat(jnp.repeat(tiles, TILE, axis=0), TILE, axis=1)
    sea_rows = lax.dynamic_slice_in_dim(sea, lax.axis_index("space") * row_count, row_count, 1)
    source = (forcing * sea_rows[None, :, :, None])[:, None]
    phase_float = phases.astype(jnp.float32)
    weight = 1.0 + 0.5 * jnp.cos(2.0 * math.pi * phase_float / PHASES)
    factors = jnp.exp(weight[None, :, None, None, None] * jnp.log(damp)[:, None])
    states = init_states
    for iteration in range(ITERS):
        field = states
        for step in range(STEPS):
            amplitude = jnp.cos(2.0 * math.pi * (phase_float * STEPS + step) / (PHASES * STEPS))[
                None, :, None, None, None
            ]
            if step % 2 == 0:
                field = column_pass(solve_x(field, inverse_x), inverse_y)
            else:
                field = solve_x(column_pass(field, inverse_y), inverse_x)
            field = vertical_mix(field, kappa_z) + amplitude * source
        offsets = field - factors * states
        own_factor = factors[:, 0]
        own_offset = offsets[:, 0]
        own = (own_factor, own_offset)
        ident = (jnp.ones_like(own_factor), jnp.zeros_like(own_offset))
        count = lax.axis_size("tm")
        here = lax.axis_index("tm")
        lower_part = ident
        upper_part = ident
        moving = jnp.stack([own_factor, own_offset])
        for turn in range(1, count):
            moving = shifted(moving, "tm", 1)
            piece = (moving[0], moving[1])
            anchor = (here - turn) % count
            before = anchor < here
            joined_low = compose(piece, lower_part)
            joined_high = compose(piece, upper_part)
            lower_part = (
                jnp.where(before, joined_low[0], lower_part[0]),
                jnp.where(before, joined_low[1], lower_part[1]),
            )
            upper_part = (
                jnp.where(before, upper_part[0], joined_high[0]),
                jnp.where(before, upper_part[1], joined_high[1]),
            )
        period = compose(compose(lower_part, own), upper_part)
        first = period[1] / (1.0 - period[0])
        start = lower_part[0] * first + lower_part[1]
        fresh = [start]
        states = jnp.stack(fresh, axis=1)
    return states


LANES = 128
HALO = 2 * ITERS
GROUPS = 1
MESH = pl.DeviceIdType.MESH


def dot(a, b):
    return jnp.dot(a, b, precision=lax.Precision.HIGHEST, preferred_element_type=jnp.float32)


def parts(a):
    high = a.astype(jnp.bfloat16)
    return high, (a - high.astype(jnp.float32)).astype(jnp.bfloat16)


def dot3(a, b):
    once = functools.partial(jnp.dot, preferred_element_type=jnp.float32)
    lines = a[0].shape[0]
    both = once(jnp.concatenate(a, axis=0), b[0])
    return both[:lines] + (once(a[0], b[1]) + both[lines:])


def iota(shape, axis):
    return lax.broadcasted_iota(jnp.int32, shape, axis)


def faces(kappa_row, n):
    row, col = iota((n, n), 0), iota((n, n), 1)
    own = jnp.sum(jnp.where(row == col, kappa_row, 0.0), axis=1, keepdims=True)
    face = 0.5 * (own + kappa_row)
    below = jnp.where(col == row - 1, face, 0.0)
    above = jnp.where(col == row + 1, face, 0.0)
    return (
        jnp.sum(below, axis=1, keepdims=True),
        jnp.sum(above, axis=1, keepdims=True),
        below + above,
    )


def reduced_inverse(kappa_row, n):
    lower, upper, _ = faces(kappa_row, n)
    shape = (n, LANES)
    a = jnp.broadcast_to(-lower, shape)
    c = jnp.broadcast_to(-upper, shape)
    b = 1.0 - a - c
    blocks = [
        (iota(shape, 0) == iota(shape, 1) + LANES * j).astype(jnp.float32)
        for j in range(max(n // LANES, 1))
    ]
    s = 1
    while s < n:
        before = functools.partial(pltpu.roll, shift=s, axis=0)
        after = functools.partial(pltpu.roll, shift=n - s, axis=0)
        alpha = -a / before(b)
        gamma = -c / after(b)
        blocks = [d + alpha * before(d) + gamma * after(d) for d in blocks]
        b = b + alpha * before(c) + gamma * after(a)
        a, c = alpha * before(a), gamma * after(c)
        s *= 2
    inverse = 1.0 / b
    return [d * inverse for d in blocks]


def copied(pick, a):
    high, low = parts(a)
    once = functools.partial(jnp.dot, preferred_element_type=jnp.float32)
    return once(pick, high) + once(pick, low)


def spread(a, pick):
    high, low = parts(a)
    once = functools.partial(jnp.dot, preferred_element_type=jnp.float32)
    return once(high, pick) + once(low, pick)


def period_kernel(
    size, u_hbm, f_hbm, damp_hbm, kx_hbm, ky_hbm, kz_hbm, sea_hbm, phase_hbm, out_ref,
    u_ref, f_ref, damp_ref, kx_ref, ky_ref, kz_ref, sea_ref, phase_ref, fetched, inverse_p,
    g_split, a_split, g_ref, a_ref, w_high, w_low, mix, ends,
    ubuf, fbuf, pbuf, xbuf, dbuf, qbuf, obuf, state, factor, source, offset_ref,
    near_out, near_in, last_out, last_in,
    u_send, u_recv, f_send, f_recv, p_send, p_recv, o_send, o_recv,
    near_send, near_recv, last_send, last_recv,
):
    n_tm, n_sp, n_t, nx, rows, nz = size
    spots = n_sp // 2
    count = n_tm * spots
    per = count // n_t
    chunk = nz // per
    window = chunk + 2 * HALO
    halves = nx // LANES
    wrows = window * rows
    crows = chunk * rows
    all_rows = spots * wrows
    tail, kept = 2 * chunk, 2 * (chunk + HALO)
    ext = LANES * -(-(all_rows + kept) // LANES)
    ny = n_sp * rows
    pieces = [(half, group) for half in range(halves) for group in range(GROUPS)]
    prows = crows // GROUPS

    here = lax.axis_index("tm")
    space = lax.axis_index("space")
    side, spot = space // spots, space % spots
    me = here * spots + spot
    across = {"tm": here, "space": (1 - side) * spots + spot}

    def window_start(k):
        return jnp.minimum(jnp.maximum(k * chunk - HALO, 0), nz - window)

    def window_rows(k):
        return pl.ds(pl.multiple_of(window_start(k) * rows, 8), wrows)

    def chunk_rows(k):
        return pl.ds(pl.multiple_of(k * crows, 8), crows)

    def device(index):
        return {"tm": index // spots, "space": side * spots + index % spots}

    pairs = (
        (u_hbm, u_ref),
        (f_hbm, f_ref),
        (damp_hbm, damp_ref),
        (kx_hbm, kx_ref),
        (ky_hbm, ky_ref),
        (kz_hbm, kz_ref),
        (sea_hbm, sea_ref),
        (phase_hbm, phase_ref),
    )
    fetches = [
        pltpu.make_async_copy(far, near, fetched.at[i]) for i, (far, near) in enumerate(pairs)
    ]
    for fetch in fetches:
        fetch.start()

    barrier = pltpu.get_barrier_semaphore()

    @pl.loop(1, count)
    def greet(offset):
        pl.semaphore_signal(
            barrier, inc=1, device_id=device((me + offset) % count), device_id_type=MESH
        )

    pl.semaphore_signal(barrier, inc=1, device_id=across, device_id_type=MESH)

    def turn(ref, buf, where):
        for t in range(n_t):
            for half in range(halves):
                for y in range(rows):
                    part = ref[t, pl.ds(half * LANES * rows + y, LANES, stride=rows), :]
                    buf[(t, *where, half, pl.ds(y, nz, stride=rows), slice(None))] = part.T

    fetches[7].wait()
    pbuf[...] = jnp.broadcast_to(phase_ref[...].astype(jnp.float32), (8, LANES))

    my_t, my_k = me // per, me % per
    my_start = window_start(my_k)

    own_u = pltpu.make_async_copy(
        ubuf.at[my_t, :, window_rows(my_k), :], xbuf.at[me], u_recv.at[here]
    )
    own_f = [
        pltpu.make_async_copy(
            fbuf.at[my_t, which, :, window_rows(my_k), :],
            dbuf.at[which, spot],
            f_recv.at[which],
        )
        for which in range(2)
    ]
    own_p = pltpu.make_async_copy(pbuf, qbuf.at[here], p_recv)

    def send_u(offset):
        index = (here ^ (offset // spots)) * spots + (spot ^ (offset % spots))
        return pltpu.make_async_remote_copy(
            src_ref=ubuf.at[index // per, :, window_rows(index % per), :],
            dst_ref=xbuf.at[here * spots + spot],
            send_sem=u_send,
            recv_sem=u_recv.at[here],
            device_id=device(index),
            device_id_type=MESH,
        )

    def send_f(which, offset):
        index = here * spots + (spot ^ (spots - offset))
        return pltpu.make_async_remote_copy(
            src_ref=fbuf.at[index // per, which, :, window_rows(index % per), :],
            dst_ref=dbuf.at[which, spot],
            send_sem=f_send,
            recv_sem=f_recv.at[which],
            device_id=device(index),
            device_id_type=MESH,
        )

    def send_p(offset):
        return pltpu.make_async_remote_copy(
            src_ref=pbuf,
            dst_ref=qbuf.at[here],
            send_sem=p_send,
            recv_sem=p_recv,
            device_id={"tm": (here + offset) % n_tm, "space": space},
            device_id_type=MESH,
        )

    def send_near(n):
        return pltpu.make_async_remote_copy(
            src_ref=near_out.at[n],
            dst_ref=near_in.at[n],
            send_sem=near_send,
            recv_sem=near_recv.at[n],
            device_id=across,
            device_id_type=MESH,
        )

    def send_last(n, piece):
        return pltpu.make_async_remote_copy(
            src_ref=last_out.at[piece, n],
            dst_ref=last_in.at[piece, n],
            send_sem=last_send,
            recv_sem=last_recv.at[piece],
            device_id=across,
            device_id_type=MESH,
        )

    def landing(piece):
        half, group = pieces[piece]
        place = pl.ds(pl.multiple_of(my_k * crows + group * prows, 8), prows)
        return out_ref.at[my_t, half, place, :]

    def send_o(piece, index):
        return pltpu.make_async_remote_copy(
            src_ref=obuf.at[piece * count + index],
            dst_ref=landing(piece),
            send_sem=o_send,
            recv_sem=o_recv,
            device_id=device(index),
            device_id_type=MESH,
        )

    fetches[0].wait()
    turn(u_ref, ubuf, ())
    pl.semaphore_wait(barrier, count)

    @pl.loop(1, n_tm)
    def start_p(offset):
        send_p(offset).start()

    far_first = [
        pair * spots + step
        for pair in (2, 3, 1, 0)
        for step in reversed(range(spots))
        if pair + step > 0
    ]
    for offset in far_first[: count // 2]:
        send_u(offset).start()

    own_p.start()
    own_u.start()
    fetches[1].wait()
    turn(f_ref, fbuf, (0,))

    @pl.loop(1, spots)
    def start_f(offset):
        send_f(0, offset).start()

    own_f[0].start()

    for offset in far_first[count // 2 :]:
        send_u(offset).start()

    fetches[2].wait()
    turn(damp_ref, fbuf, (1,))

    for fetch in fetches[3:7]:
        fetch.wait()

    for half, block in enumerate(reduced_inverse(kx_ref[...], nx)):
        a_ref[:, half * LANES : (half + 1) * LANES] = block
    a_once = a_ref[...]
    for i, part in enumerate(parts(a_once)):
        a_split[0, i] = part
    for i, part in enumerate(parts(dot(a_once, a_once))):
        a_split[1, i] = part

    inverse_y = reduced_inverse(ky_ref[...], ny)[0]
    row, col = iota((ny, LANES), 0), iota((ny, LANES), 1)
    edge, far_edge = ny // 2 - 1 + side, ny // 2 - side
    own_row, own_col = row // (ny // 2) == side, col // (ny // 2) == side
    inner_y = jnp.where(own_row & own_col, inverse_y, 0.0)
    twice_y = dot(inverse_y[:, :ny], inverse_y)
    inner_twice = dot(inner_y[:, :ny], inner_y)
    corner = jnp.sum(
        jnp.sum(
            jnp.where((row == far_edge) & (col == far_edge), inverse_y, 0.0), axis=1, keepdims=True
        ),
        axis=0,
        keepdims=True,
    )
    leave_once = jnp.sum(jnp.where(row == edge, inner_y, 0.0), axis=0, keepdims=True)
    leave_twice = jnp.sum(jnp.where(row == edge, inner_twice, 0.0), axis=0, keepdims=True)
    enter_line = (
        jnp.sum(jnp.where((row == far_edge) & own_col, inverse_y, 0.0), axis=0, keepdims=True)
        / corner
    )
    enter_once = (
        jnp.sum(jnp.where((col == far_edge) & own_row, inverse_y, 0.0), axis=1, keepdims=True)
        / corner
    )
    enter_twice = jnp.sum(inner_y * enter_line, axis=1, keepdims=True)
    below = iota((ny, LANES), 0)
    ext_y_once = jnp.concatenate(
        [
            inverse_y + jnp.where(col == ny, enter_once, 0.0),
            jnp.where(below == 0, leave_once, 0.0),
        ],
        axis=0,
    )
    ext_y_twice = jnp.concatenate(
        [
            twice_y
            + jnp.where(col == ny, enter_twice, 0.0)
            + jnp.where(col == ny + 1, enter_once, 0.0),
            jnp.where(below == 0, leave_once, jnp.where(below == 1, leave_twice, 0.0)),
        ],
        axis=0,
    )

    def line_of(q):
        own = side * (ny // 2) + (q // wrows) * rows + q % rows
        return jnp.where(q < all_rows, own, ny + q % 2)

    def level_of(q):
        own = my_start + (q % wrows) // rows
        p = (q - all_rows) // 2
        first = my_k * chunk
        ring = jnp.where(p < chunk + HALO // 2, first - HALO // 2 - chunk, first - HALO // 2) + p
        passed = jnp.where(p < chunk, first + p, ring)
        return jnp.where(q < all_rows, own, jnp.where(q < all_rows + kept, passed, -1))

    def mask(a, b):
        return jnp.where(a == b, 1.0, 0.0).astype(jnp.bfloat16)

    pick_y = mask(line_of(iota((ext, 2 * ny), 0)), iota((ext, 2 * ny), 1))
    pick_y_back = mask(line_of(iota((LANES, ext), 1)), iota((LANES, ext), 0))
    pick_z = mask(level_of(iota((ext, nz), 0)), iota((ext, nz), 1))
    pick_z_back = mask(level_of(iota((nz, ext), 1)), iota((nz, ext), 0))
    own_columns = iota((nz, ext), 1) < all_rows
    _, _, beside = faces(kz_ref[...], nz)
    identity = (iota((nz, nz), 0) == iota((nz, nz), 1)).astype(jnp.float32)
    vertical = beside + identity * (1.0 - jnp.sum(beside, axis=1, keepdims=True))
    for order, (ext_y, mixed) in enumerate(
        ((ext_y_once, vertical), (ext_y_twice, dot(vertical, vertical)))
    ):
        across_y = spread(copied(pick_y, ext_y), pick_y_back)
        levels = jnp.where(own_columns, spread(mixed, pick_z_back), pick_z_back.astype(jnp.float32))
        whole = across_y * copied(pick_z, levels)
        for i, part in enumerate(parts(whole)):
            g_split[order, i] = part
    g_ref[...] = whole
    inner = (my_k * chunk - my_start) * rows

    def inner_rows(r):
        return pl.ds(pl.multiple_of(r * wrows + inner, 8), crows)

    inner_g = jnp.concatenate([g_ref[inner_rows(r), :] for r in range(spots)], axis=0)
    inner_g = jnp.where(iota((spots * crows, ext), 1) < all_rows, inner_g, 0.0)
    for i, part in enumerate(parts(inner_g)):
        g_split[2, i, : spots * crows, :] = part
    q = iota((spots * prows, LANES), 0)
    picked = side * (ny // 2) + (q // prows) * rows + q % rows
    picked = jnp.where(picked == iota((spots * prows, LANES), 1), 1.0, 0.0)[:, :ny]
    enters = [dot(picked, jnp.broadcast_to(c, (ny, LANES))) for c in (enter_twice, enter_once)]
    mix[0] = jnp.where(q % 2 == 0, enters[0], enters[1])
    mix[1] = jnp.where(q % 2 == 0, enters[1], enters[0])

    w_high[:, all_rows:, :] = jnp.zeros((n_tm + 1, ext - all_rows, nx), jnp.bfloat16)
    w_low[:, all_rows:, :] = jnp.zeros((n_tm + 1, ext - all_rows, nx), jnp.bfloat16)

    tile = (iota((nx // TILE, nx), 1) // TILE == iota((nx // TILE, nx), 0)).astype(jnp.float32)
    tiles = nx // TILE
    flags = jnp.where(
        iota((tiles, tiles), 0) == iota((tiles, tiles), 1), sea_ref[...].astype(jnp.float32), 0.0
    )
    sea = jnp.sum(jnp.sum(flags, axis=1, keepdims=True) * tile, axis=0, keepdims=True)

    def gathered(ref, where):
        return jnp.concatenate(
            [ref[where(half)].reshape(all_rows, LANES) for half in range(halves)], axis=1
        )

    def solve_x_lines(n, order, field):
        moved = dot3(parts(field), (a_split[order, 0], a_split[order, 1]))
        w_high[n, :all_rows, :], w_low[n, :all_rows, :] = parts(moved)

    def leaving(n, order, lines):
        padded = 16 * -(-lines // 16)
        block = slice(all_rows, all_rows + padded)
        found = dot3(
            (g_split[order, 0, block, :], g_split[order, 1, block, :]), (w_high[n], w_low[n])
        )
        return found[:lines]

    def joined(n, order):
        w_high[n, all_rows:, :], w_low[n, all_rows:, :] = parts(
            jnp.concatenate(
                [near_in[n], jnp.zeros((ext - all_rows - kept, nx), jnp.float32)], axis=0
            )
        )
        block = slice(0, all_rows)
        return dot3(
            (g_split[order, 0, block, :], g_split[order, 1, block, :]), (w_high[n], w_low[n])
        )

    def slab_of(n):
        return xbuf.at[pl.ds(n * spots, spots)]

    def arrive_u(turned):
        n = here ^ ((turned + 1) % n_tm)

        slot = slab_of(n)
        pltpu.make_async_copy(slot, slot, u_recv.at[n]).wait()
        solve_x_lines(n, 1, gathered(xbuf, lambda half: (pl.ds(n * spots, spots), half)))
        near_out[n] = leaving(n, 1, kept)
        send_near(n).start()

    arrive_u(1)

    @pl.loop(1, spots)
    def start_damp(offset):
        send_f(1, offset).start()

    own_f[1].start()

    arrive_u(2)

    pltpu.make_async_copy(dbuf.at[0], dbuf.at[0], f_recv.at[0]).wait()

    source[1] = gathered(dbuf, lambda half: (0, slice(None), half)) * sea
    solve_x_lines(n_tm, 0, source[1])
    near_out[n_tm] = leaving(n_tm, 0, kept)
    send_near(n_tm).start()

    pl.loop(n_tm // 2 + 1, n_tm + 1)(arrive_u)

    pltpu.make_async_copy(qbuf, qbuf, p_recv).wait()
    pltpu.make_async_copy(dbuf.at[1], dbuf.at[1], f_recv.at[1]).wait()

    def wide(values):
        return jnp.concatenate([values[:1]] * halves, axis=1)

    log_damp = jnp.log(gathered(dbuf, lambda half: (1, slice(None), half)))
    product = None
    for n in range(n_tm):
        weight = 1.0 + 0.5 * jnp.cos(2.0 * math.pi * qbuf[n] / PHASES)
        one = jnp.exp(wide(weight) * log_damp)
        factor[n] = one
        product = one if product is None else one * product
    inverse_p[...] = 1.0 / (1.0 - product)

    def wait_near(n):
        pltpu.make_async_copy(near_in.at[n], near_in.at[n], near_recv.at[n]).wait()

    away = xbuf.at[pl.ds(0, count - 1)]
    pltpu.make_async_copy(away, away, u_send).wait()
    away = dbuf.at[:, pl.ds(0, spots - 1)]
    pltpu.make_async_copy(away, away, f_send).wait()
    away = qbuf.at[pl.ds(0, n_tm - 1)]
    pltpu.make_async_copy(away, away, p_send).wait()
    wait_near(n_tm)
    source[0] = joined(n_tm, 0)

    @pl.loop(0, n_tm)
    def make_offsets(n):
        phase = qbuf[n]
        first = jnp.cos(2.0 * math.pi * (phase * STEPS) / (PHASES * STEPS))
        second = jnp.cos(2.0 * math.pi * (phase * STEPS + 1) / (PHASES * STEPS))
        offset_ref[n] = wide(first) * source[0] + wide(second) * source[1]

    @pl.loop(1, n_tm + 1)
    def finish_first(turned):
        n = here ^ ((turned + 1) % n_tm)
        wait_near(n)
        field = gathered(xbuf, lambda half: (pl.ds(n * spots, spots), half))
        state[n] = joined(n, 1) + offset_ref[n] - factor[n] * field

    def solve_first(r):
        block = pl.ds(pl.multiple_of(r * wrows, 8), wrows)
        factors = [factor[n, block, :] for n in range(n_tm)]
        offsets = [state[n, block, :] for n in range(n_tm)]
        total = offsets[0]
        for n in range(1, n_tm):
            total = factors[n] * total + offsets[n]
        fresh = total * inverse_p[block, :]
        for n in range(n_tm):
            state[n, block, :] = fresh
            fresh = factors[n] * fresh + offsets[n]

    for r in range(spots):
        solve_first(r)

    def lanes(half):
        return slice(half * LANES, (half + 1) * LANES)

    first_pieces = 1

    a_twice = a_split[1, 0], a_split[1, 1]
    picked_rows = []
    for n in range(n_tm):
        w_high[n, :all_rows, :], w_low[n, :all_rows, :] = parts(state[n])
        picked_rows.append(leaving(n, 1, tail))
    found = dot3(parts(jnp.concatenate(picked_rows, axis=0)), a_twice)
    for n in range(n_tm):
        for piece, (half, group) in enumerate(pieces):
            first = n * tail + group * prows
            last_out[piece, n] = found[first : first + prows, lanes(half)]
        for piece in range(first_pieces):
            send_last(n, piece).start()

    for piece in range(first_pieces, len(pieces)):

        @pl.loop(0, n_tm)
        def start_last(n):
            send_last(n, piece).start()

    pltpu.make_async_copy(near_in, near_in, near_send).wait()

    def own_last(n):
        upper = slice(0, spots * crows)
        own = dot3(
            (g_split[2, 0, upper, :], g_split[2, 1, upper, :]), (w_high[n], w_low[n])
        )
        own = dot3(parts(own), a_twice)
        for r in range(spots):
            packed = slice(r * crows, (r + 1) * crows)
            block = inner_rows(r)
            ends[n, packed, :] = (
                own[packed] + offset_ref[n, block, :] - factor[n, block, :] * state[n, block, :]
            )

    for n in range(n_tm):
        own_last(n)

    even = iota((prows, LANES), 0) % 2 == 0

    def swapped(a):
        return jnp.where(even, pltpu.roll(a, prows - 1, 0), pltpu.roll(a, 1, 0))

    for piece, (half, group) in enumerate(pieces):
        slot = last_in.at[piece]
        pltpu.make_async_copy(slot, slot, last_recv.at[piece]).wait()

        def solve_last(turned):
            r = (spot + turned) % spots
            block = pl.ds(pl.multiple_of(r * wrows + inner + group * prows, 8), prows)
            packed = pl.ds(pl.multiple_of(r * crows + group * prows, 8), prows)
            mine = pl.ds(pl.multiple_of(r * prows, 8), prows)
            factors = [factor[n, block, lanes(half)] for n in range(n_tm)]
            offsets = []
            for n in range(n_tm):
                entering = last_in[piece, n]
                offsets.append(
                    ends[n, packed, lanes(half)]
                    + mix[0, mine, :] * entering
                    + mix[1, mine, :] * swapped(entering)
                )
            total = offsets[0]
            for n in range(1, n_tm):
                total = factors[n] * total + offsets[n]
            fresh = total * inverse_p[block, lanes(half)]
            for n in range(n_tm):
                obuf[piece * count + n * spots + r] = fresh
                fresh = factors[n] * fresh + offsets[n]
            for n in range(n_tm):

                @pl.when(n * spots + r != me)
                def _():
                    send_o(piece, n * spots + r).start()

        for turned in range(1, spots + 1):
            solve_last(turned)
        pltpu.make_async_copy(obuf.at[piece * count + me], landing(piece), o_recv).start()

    pltpu.make_async_copy(last_in, last_in, last_send).wait()
    pltpu.make_async_copy(out_ref, out_ref, o_recv).wait()
    away = obuf.at[pl.ds(0, len(pieces) * (count - 1))]
    pltpu.make_async_copy(away, away, o_send).wait()


def turn_kernel(size, in_ref, out_ref, near_ref, turned_ref, in_sem, out_sem):
    n_t, halves, rows, nz = size
    blocks = [(t, half) for half in range(halves) for t in range(n_t)]

    def fetch(i):
        return pltpu.make_async_copy(in_ref.at[blocks[i]], near_ref.at[i], in_sem.at[i])

    def store(i):
        t, half = blocks[i]
        place = pl.ds(half * LANES * rows, LANES * rows)
        return pltpu.make_async_copy(turned_ref.at[i], out_ref.at[t, place, :], out_sem.at[i])

    for i in range(len(blocks)):
        fetch(i).start()
    for i in range(len(blocks)):
        fetch(i).wait()
        for y in range(rows):
            part = near_ref[i, pl.ds(y, nz, stride=rows), :]
            turned_ref[i, pl.ds(y, LANES, stride=rows), :] = part.T
        store(i).start()
    for i in range(len(blocks)):
        store(i).wait()


def whole_period(init_states, forcing, damp, kappa_x, kappa_y, kappa_z, sea_tiles, phases):
    n_tm, n_sp = lax.axis_size("tm"), lax.axis_size("space")
    n_t, _, nx, rows, nz = init_states.shape
    spots = n_sp // 2
    count = n_tm * spots
    chunk = nz // (count // n_t)
    window = chunk + 2 * HALO
    halves = nx // LANES
    wrows = window * rows
    crows = chunk * rows
    all_rows = spots * wrows
    kept = 2 * (chunk + HALO)
    prows = crows // GROUPS
    ext = LANES * -(-(all_rows + kept) // LANES)
    flat = (n_t, nx * rows, nz)
    f32 = jnp.float32
    bf16 = jnp.bfloat16
    landed = pl.pallas_call(
        functools.partial(period_kernel, (n_tm, n_sp, n_t, nx, rows, nz)),
        out_shape=jax.ShapeDtypeStruct((n_t, halves, nz * rows, LANES), f32),
        in_specs=[pl.BlockSpec(memory_space=pltpu.HBM)] * 8,
        out_specs=pl.BlockSpec(memory_space=pltpu.HBM),
        scratch_shapes=[
            pltpu.VMEM(flat, f32),
            pltpu.VMEM(flat, f32),
            pltpu.VMEM(flat, f32),
            pltpu.VMEM((1, nx), f32),
            pltpu.VMEM((1, kappa_y.shape[0]), f32),
            pltpu.VMEM((1, nz), f32),
            pltpu.VMEM((1, sea_tiles.shape[0]), jnp.int32),
            pltpu.VMEM((1, 1), jnp.int32),
            pltpu.SemaphoreType.DMA((8,)),
            pltpu.VMEM((all_rows, nx), f32),
            pltpu.VMEM((3, 2, ext, ext), bf16),
            pltpu.VMEM((2, 2, nx, nx), bf16),
            pltpu.VMEM((ext, ext), f32),
            pltpu.VMEM((nx, nx), f32),
            pltpu.VMEM((n_tm + 1, ext, nx), bf16),
            pltpu.VMEM((n_tm + 1, ext, nx), bf16),
            pltpu.VMEM((2, spots * prows, LANES), f32),
            pltpu.VMEM((n_tm, spots * crows, nx), f32),
            pltpu.VMEM((n_t, halves, nz * rows, LANES), f32),
            pltpu.VMEM((n_t, 2, halves, nz * rows, LANES), f32),
            pltpu.VMEM((8, LANES), f32),
            pltpu.VMEM((count, halves, wrows, LANES), f32),
            pltpu.VMEM((2, spots, halves, wrows, LANES), f32),
            pltpu.VMEM((n_tm, 8, LANES), f32),
            pltpu.VMEM((halves * GROUPS * count, prows, LANES), f32),
            pltpu.VMEM((n_tm, all_rows, nx), f32),
            pltpu.VMEM((n_tm, all_rows, nx), f32),
            pltpu.VMEM((2, all_rows, nx), f32),
            pltpu.VMEM((n_tm, all_rows, nx), f32),
            pltpu.VMEM((n_tm + 1, kept, nx), f32),
            pltpu.VMEM((n_tm + 1, kept, nx), f32),
            pltpu.VMEM((halves * GROUPS, n_tm, prows, LANES), f32),
            pltpu.VMEM((halves * GROUPS, n_tm, prows, LANES), f32),
            pltpu.SemaphoreType.DMA,
            pltpu.SemaphoreType.DMA((n_tm,)),
            pltpu.SemaphoreType.DMA,
            pltpu.SemaphoreType.DMA((2,)),
            pltpu.SemaphoreType.DMA,
            pltpu.SemaphoreType.DMA,
            pltpu.SemaphoreType.DMA,
            pltpu.SemaphoreType.DMA,
            pltpu.SemaphoreType.DMA,
            pltpu.SemaphoreType.DMA((n_tm + 1,)),
            pltpu.SemaphoreType.DMA,
            pltpu.SemaphoreType.DMA((halves * GROUPS,)),
        ],
        compiler_params=pltpu.CompilerParams(
            collective_id=0, has_side_effects=True, vmem_limit_bytes=63 * 1024 * 1024
        ),
    )(
        init_states.reshape(flat),
        forcing.reshape(flat),
        damp.reshape(flat),
        kappa_x[None],
        kappa_y[None],
        kappa_z[None],
        sea_tiles.reshape(1, -1),
        phases.reshape(1, 1),
    )
    pieces = n_t * halves
    out = pl.pallas_call(
        functools.partial(turn_kernel, (n_t, halves, rows, nz)),
        out_shape=jax.ShapeDtypeStruct(flat, f32),
        in_specs=[pl.BlockSpec(memory_space=pl.ANY)],
        out_specs=pl.BlockSpec(memory_space=pl.ANY),
        scratch_shapes=[
            pltpu.VMEM((pieces, nz * rows, LANES), f32),
            pltpu.VMEM((pieces, LANES * rows, nz), f32),
            pltpu.SemaphoreType.DMA((pieces,)),
            pltpu.SemaphoreType.DMA((pieces,)),
        ],
    )(landed)
    return out.reshape(init_states.shape)


def choose(init_states, forcing, damp, kappa_x, kappa_y, kappa_z, sea_tiles, phases):
    spots = lax.axis_size("space") // 2
    count = lax.axis_size("tm") * spots
    n_t, slabs, nx, rows, nz = init_states.shape
    ny = lax.axis_size("space") * rows
    per = max(count // n_t, 1)
    chunk = nz // per
    all_rows = spots * (chunk + 2 * HALO) * rows
    fits = (
        ITERS == 2
        and slabs == 1
        and lax.axis_size("space") % 2 == 0
        and lax.axis_size("tm") == 4
        and spots & (spots - 1) == 0
        and count % n_t == 0
        and nz == LANES
        and nx % LANES == 0
        and nz % per == 0
        and rows == 2
        and chunk * rows % (8 * GROUPS) == 0
        and HALO * rows % 8 == 0
        and HALO <= chunk
        and chunk % 8 == 0
        and all_rows % 16 == 0
        and chunk + 2 * HALO <= nz
        and ny + 2 <= LANES
        and ny & (ny - 1) == 0
        and ny >= 16
        and sea_tiles.shape[1] == 1
        and all_rows + 2 * (chunk + HALO) <= 512
    )
    run = whole_period if fits else body
    return run(init_states, forcing, damp, kappa_x, kappa_y, kappa_z, sea_tiles, phases)


def solution(mesh):
    return jax.shard_map(
        choose,
        mesh=mesh,
        in_specs=(
            P(None, "tm", None, "space", None),
            P(None, None, "space", None),
            P(None, None, "space", None),
            P(),
            P(),
            P(),
            P(),
            P("tm"),
        ),
        out_specs=P(None, "tm", None, "space", None),
        check_vma=False,
    )
```

```python
import functools
import math

import jax
import jax.numpy as jnp
from jax import lax
from jax.experimental import pallas as pl
from jax.experimental.pallas import tpu as pltpu
from jax.sharding import PartitionSpec as P

STEPS = 2
ITERS = 2
TILE = 16
PHASES = 12


def shifted(array, axis, by):
    devices = lax.axis_size(axis)
    return lax.ppermute(array, axis, [(i, (i + by) % devices) for i in range(devices)])


def line_inverse(kappa):
    face = 0.5 * (kappa[1:] + kappa[:-1])
    zero = jnp.zeros((1,), kappa.dtype)
    left = jnp.concatenate([zero, face])
    right = jnp.concatenate([face, zero])
    identity = jnp.eye(kappa.shape[0], dtype=kappa.dtype)
    return lax.linalg.tridiagonal_solve(-left, 1.0 + left + right, -right, identity)


def solve_lines(field, inverse):
    return jnp.matmul(inverse, field, precision=lax.Precision.HIGHEST)


def solve_x(field, inverse):
    shape = field.shape
    flat = field.reshape(shape[0], shape[1], shape[2], shape[3] * shape[4])
    return solve_lines(flat, inverse).reshape(shape)


def vertical_mix(field, kappa_z):
    face = 0.5 * (kappa_z[1:] + kappa_z[:-1])
    flux = face * (field[..., 1:] - field[..., :-1])
    zeros = jnp.zeros(field.shape[:-1] + (1,), field.dtype)
    flux = jnp.concatenate([zeros, flux, zeros], axis=-1)
    return field + flux[..., 1:] - flux[..., :-1]


def compose(earlier, later):
    return (earlier[0] * later[0], later[0] * earlier[1] + later[1])


def column_pass(field, inverse_y):
    return lax.all_to_all(
        solve_lines(
            lax.all_to_all(field, "space", split_axis=2, concat_axis=3, tiled=True), inverse_y
        ),
        "space",
        split_axis=3,
        concat_axis=2,
        tiled=True,
    )


def body(init_states, forcing, damp, kappa_x, kappa_y, kappa_z, sea_tiles, phases):
    row_count = init_states.shape[3]
    inverse_x = line_inverse(kappa_x)
    inverse_y = line_inverse(kappa_y)
    tiles = sea_tiles.astype(jnp.float32)
    sea = jnp.repeat(jnp.repeat(tiles, TILE, axis=0), TILE, axis=1)
    sea_rows = lax.dynamic_slice_in_dim(sea, lax.axis_index("space") * row_count, row_count, 1)
    source = (forcing * sea_rows[None, :, :, None])[:, None]
    phase_float = phases.astype(jnp.float32)
    weight = 1.0 + 0.5 * jnp.cos(2.0 * math.pi * phase_float / PHASES)
    factors = jnp.exp(weight[None, :, None, None, None] * jnp.log(damp)[:, None])
    states = init_states
    for iteration in range(ITERS):
        field = states
        for step in range(STEPS):
            amplitude = jnp.cos(2.0 * math.pi * (phase_float * STEPS + step) / (PHASES * STEPS))[
                None, :, None, None, None
            ]
            if step % 2 == 0:
                field = column_pass(solve_x(field, inverse_x), inverse_y)
            else:
                field = solve_x(column_pass(field, inverse_y), inverse_x)
            field = vertical_mix(field, kappa_z) + amplitude * source
        offsets = field - factors * states
        own_factor = factors[:, 0]
        own_offset = offsets[:, 0]
        own = (own_factor, own_offset)
        ident = (jnp.ones_like(own_factor), jnp.zeros_like(own_offset))
        count = lax.axis_size("tm")
        here = lax.axis_index("tm")
        lower_part = ident
        upper_part = ident
        moving = jnp.stack([own_factor, own_offset])
        for turn in range(1, count):
            moving = shifted(moving, "tm", 1)
            piece = (moving[0], moving[1])
            anchor = (here - turn) % count
            before = anchor < here
            joined_low = compose(piece, lower_part)
            joined_high = compose(piece, upper_part)
            lower_part = (
                jnp.where(before, joined_low[0], lower_part[0]),
                jnp.where(before, joined_low[1], lower_part[1]),
            )
            upper_part = (
                jnp.where(before, upper_part[0], joined_high[0]),
                jnp.where(before, upper_part[1], joined_high[1]),
            )
        period = compose(compose(lower_part, own), upper_part)
        first = period[1] / (1.0 - period[0])
        start = lower_part[0] * first + lower_part[1]
        fresh = [start]
        states = jnp.stack(fresh, axis=1)
    return states


LANES = 128
HALO = 2 * ITERS
GROUPS = 1
MESH = pl.DeviceIdType.MESH


def dot(a, b):
    return jnp.dot(a, b, precision=lax.Precision.HIGHEST, preferred_element_type=jnp.float32)


def parts(a):
    high = a.astype(jnp.bfloat16)
    return high, (a - high.astype(jnp.float32)).astype(jnp.bfloat16)


def dot3(a, b):
    once = functools.partial(jnp.dot, preferred_element_type=jnp.float32)
    lines = a[0].shape[0]
    both = once(jnp.concatenate(a, axis=0), b[0])
    return both[:lines] + (once(a[0], b[1]) + both[lines:])


def iota(shape, axis):
    return lax.broadcasted_iota(jnp.int32, shape, axis)


def faces(kappa_row, n):
    row, col = iota((n, n), 0), iota((n, n), 1)
    own = jnp.sum(jnp.where(row == col, kappa_row, 0.0), axis=1, keepdims=True)
    face = 0.5 * (own + kappa_row)
    below = jnp.where(col == row - 1, face, 0.0)
    above = jnp.where(col == row + 1, face, 0.0)
    return (
        jnp.sum(below, axis=1, keepdims=True),
        jnp.sum(above, axis=1, keepdims=True),
        below + above,
    )


def reduced_inverse(kappa_row, n):
    lower, upper, _ = faces(kappa_row, n)
    shape = (n, LANES)
    a = jnp.broadcast_to(-lower, shape)
    c = jnp.broadcast_to(-upper, shape)
    b = 1.0 - a - c
    blocks = [
        (iota(shape, 0) == iota(shape, 1) + LANES * j).astype(jnp.float32)
        for j in range(max(n // LANES, 1))
    ]
    s = 1
    while s < n:
        before = functools.partial(pltpu.roll, shift=s, axis=0)
        after = functools.partial(pltpu.roll, shift=n - s, axis=0)
        alpha = -a / before(b)
        gamma = -c / after(b)
        blocks = [d + alpha * before(d) + gamma * after(d) for d in blocks]
        b = b + alpha * before(c) + gamma * after(a)
        a, c = alpha * before(a), gamma * after(c)
        s *= 2
    inverse = 1.0 / b
    return [d * inverse for d in blocks]


def copied(pick, a):
    high, low = parts(a)
    once = functools.partial(jnp.dot, preferred_element_type=jnp.float32)
    return once(pick, high) + once(pick, low)


def spread(a, pick):
    high, low = parts(a)
    once = functools.partial(jnp.dot, preferred_element_type=jnp.float32)
    return once(high, pick) + once(low, pick)


def period_kernel(
    size, u_hbm, f_hbm, damp_hbm, kx_hbm, ky_hbm, kz_hbm, sea_hbm, phase_hbm, out_ref,
    u_ref, f_ref, damp_ref, kx_ref, ky_ref, kz_ref, sea_ref, phase_ref, fetched, inverse_p,
    g_split, a_split, g_ref, a_ref, w_high, w_low, mix, ends,
    ubuf, fbuf, pbuf, xbuf, dbuf, qbuf, obuf, state, factor, source, offset_ref,
    near_out, near_in, last_out, last_in,
    u_send, u_recv, f_send, f_recv, p_send, p_recv, o_send, o_recv,
    near_send, near_recv, last_send, last_recv,
):
    n_tm, n_sp, n_t, nx, rows, nz = size
    spots = n_sp // 2
    count = n_tm * spots
    per = count // n_t
    chunk = nz // per
    window = chunk + 2 * HALO
    halves = nx // LANES
    wrows = window * rows
    crows = chunk * rows
    all_rows = spots * wrows
    tail, kept = 2 * chunk, 2 * (chunk + HALO)
    ext = LANES * -(-(all_rows + kept) // LANES)
    ny = n_sp * rows
    pieces = [(half, group) for half in range(halves) for group in range(GROUPS)]
    prows = crows // GROUPS

    here = lax.axis_index("tm")
    space = lax.axis_index("space")
    side, spot = space // spots, space % spots
    me = here * spots + spot
    across = {"tm": here, "space": (1 - side) * spots + spot}

    def window_start(k):
        return jnp.minimum(jnp.maximum(k * chunk - HALO, 0), nz - window)

    def window_rows(k):
        return pl.ds(pl.multiple_of(window_start(k) * rows, 8), wrows)

    def chunk_rows(k):
        return pl.ds(pl.multiple_of(k * crows, 8), crows)

    def device(index):
        return {"tm": index // spots, "space": side * spots + index % spots}

    pairs = (
        (u_hbm, u_ref),
        (f_hbm, f_ref),
        (damp_hbm, damp_ref),
        (kx_hbm, kx_ref),
        (ky_hbm, ky_ref),
        (kz_hbm, kz_ref),
        (sea_hbm, sea_ref),
        (phase_hbm, phase_ref),
    )
    fetches = [
        pltpu.make_async_copy(far, near, fetched.at[i]) for i, (far, near) in enumerate(pairs)
    ]
    for fetch in fetches:
        fetch.start()

    barrier = pltpu.get_barrier_semaphore()

    @pl.loop(1, count)
    def greet(offset):
        pl.semaphore_signal(
            barrier, inc=1, device_id=device((me + offset) % count), device_id_type=MESH
        )

    pl.semaphore_signal(barrier, inc=1, device_id=across, device_id_type=MESH)

    def turn(ref, buf, where):
        for t in range(n_t):
            for half in range(halves):
                for y in range(rows):
                    part = ref[t, pl.ds(half * LANES * rows + y, LANES, stride=rows), :]
                    buf[(t, *where, half, pl.ds(y, nz, stride=rows), slice(None))] = part.T

    fetches[7].wait()
    pbuf[...] = jnp.broadcast_to(phase_ref[...].astype(jnp.float32), (8, LANES))

    my_t, my_k = me // per, me % per
    my_start = window_start(my_k)

    own_u = pltpu.make_async_copy(
        ubuf.at[my_t, :, window_rows(my_k), :], xbuf.at[me], u_recv.at[here]
    )
    own_f = [
        pltpu.make_async_copy(
            fbuf.at[my_t, which, :, window_rows(my_k), :],
            dbuf.at[which, spot],
            f_recv.at[which],
        )
        for which in range(2)
    ]
    own_p = pltpu.make_async_copy(pbuf, qbuf.at[here], p_recv)

    def send_u(offset):
        index = (here ^ (offset // spots)) * spots + (spot ^ (offset % spots))
        return pltpu.make_async_remote_copy(
            src_ref=ubuf.at[index // per, :, window_rows(index % per), :],
            dst_ref=xbuf.at[here * spots + spot],
            send_sem=u_send,
            recv_sem=u_recv.at[here],
            device_id=device(index),
            device_id_type=MESH,
        )

    def send_f(which, offset):
        index = here * spots + (spot ^ (spots - offset))
        return pltpu.make_async_remote_copy(
            src_ref=fbuf.at[index // per, which, :, window_rows(index % per), :],
            dst_ref=dbuf.at[which, spot],
            send_sem=f_send,
            recv_sem=f_recv.at[which],
            device_id=device(index),
            device_id_type=MESH,
        )

    def send_p(offset):
        return pltpu.make_async_remote_copy(
            src_ref=pbuf,
            dst_ref=qbuf.at[here],
            send_sem=p_send,
            recv_sem=p_recv,
            device_id={"tm": (here + offset) % n_tm, "space": space},
            device_id_type=MESH,
        )

    def send_near(n):
        return pltpu.make_async_remote_copy(
            src_ref=near_out.at[n],
            dst_ref=near_in.at[n],
            send_sem=near_send,
            recv_sem=near_recv.at[n],
            device_id=across,
            device_id_type=MESH,
        )

    def send_last(n, piece):
        return pltpu.make_async_remote_copy(
            src_ref=last_out.at[piece, n],
            dst_ref=last_in.at[piece, n],
            send_sem=last_send,
            recv_sem=last_recv.at[piece],
            device_id=across,
            device_id_type=MESH,
        )

    def landing(piece):
        half, group = pieces[piece]
        place = pl.ds(pl.multiple_of(my_k * crows + group * prows, 8), prows)
        return out_ref.at[my_t, half, place, :]

    def send_o(piece, index):
        return pltpu.make_async_remote_copy(
            src_ref=obuf.at[piece * count + index],
            dst_ref=landing(piece),
            send_sem=o_send,
            recv_sem=o_recv,
            device_id=device(index),
            device_id_type=MESH,
        )

    fetches[0].wait()
    turn(u_ref, ubuf, ())
    pl.semaphore_wait(barrier, count)

    @pl.loop(1, n_tm)
    def start_p(offset):
        send_p(offset).start()

    far_first = [
        pair * spots + step
        for pair in (2, 3, 1, 0)
        for step in reversed(range(spots))
        if pair + step > 0
    ]
    for offset in far_first[: count // 2]:
        send_u(offset).start()

    own_p.start()
    own_u.start()
    fetches[1].wait()
    turn(f_ref, fbuf, (0,))

    @pl.loop(1, spots)
    def start_f(offset):
        send_f(0, offset).start()

    own_f[0].start()

    for offset in far_first[count // 2 :]:
        send_u(offset).start()

    fetches[2].wait()
    turn(damp_ref, fbuf, (1,))

    for fetch in fetches[3:7]:
        fetch.wait()

    for half, block in enumerate(reduced_inverse(kx_ref[...], nx)):
        a_ref[:, half * LANES : (half + 1) * LANES] = block
    a_once = a_ref[...]
    for i, part in enumerate(parts(a_once)):
        a_split[0, i] = part
    for i, part in enumerate(parts(dot(a_once, a_once))):
        a_split[1, i] = part

    inverse_y = reduced_inverse(ky_ref[...], ny)[0]
    row, col = iota((ny, LANES), 0), iota((ny, LANES), 1)
    edge, far_edge = ny // 2 - 1 + side, ny // 2 - side
    own_row, own_col = row // (ny // 2) == side, col // (ny // 2) == side
    inner_y = jnp.where(own_row & own_col, inverse_y, 0.0)
    twice_y = dot(inverse_y[:, :ny], inverse_y)
    inner_twice = dot(inner_y[:, :ny], inner_y)
    corner = jnp.sum(
        jnp.sum(
            jnp.where((row == far_edge) & (col == far_edge), inverse_y, 0.0), axis=1, keepdims=True
        ),
        axis=0,
        keepdims=True,
    )
    leave_once = jnp.sum(jnp.where(row == edge, inner_y, 0.0), axis=0, keepdims=True)
    leave_twice = jnp.sum(jnp.where(row == edge, inner_twice, 0.0), axis=0, keepdims=True)
    enter_line = (
        jnp.sum(jnp.where((row == far_edge) & own_col, inverse_y, 0.0), axis=0, keepdims=True)
        / corner
    )
    enter_once = (
        jnp.sum(jnp.where((col == far_edge) & own_row, inverse_y, 0.0), axis=1, keepdims=True)
        / corner
    )
    enter_twice = jnp.sum(inner_y * enter_line, axis=1, keepdims=True)
    below = iota((ny, LANES), 0)
    ext_y_once = jnp.concatenate(
        [
            inverse_y + jnp.where(col == ny, enter_once, 0.0),
            jnp.where(below == 0, leave_once, 0.0),
        ],
        axis=0,
    )
    ext_y_twice = jnp.concatenate(
        [
            twice_y
            + jnp.where(col == ny, enter_twice, 0.0)
            + jnp.where(col == ny + 1, enter_once, 0.0),
            jnp.where(below == 0, leave_once, jnp.where(below == 1, leave_twice, 0.0)),
        ],
        axis=0,
    )

    def line_of(q):
        own = side * (ny // 2) + (q // wrows) * rows + q % rows
        return jnp.where(q < all_rows, own, ny + q % 2)

    def level_of(q):
        own = my_start + (q % wrows) // rows
        p = (q - all_rows) // 2
        first = my_k * chunk
        ring = jnp.where(p < chunk + HALO // 2, first - HALO // 2 - chunk, first - HALO // 2) + p
        passed = jnp.where(p < chunk, first + p, ring)
        return jnp.where(q < all_rows, own, jnp.where(q < all_rows + kept, passed, -1))

    def mask(a, b):
        return jnp.where(a == b, 1.0, 0.0).astype(jnp.bfloat16)

    pick_y = mask(line_of(iota((ext, 2 * ny), 0)), iota((ext, 2 * ny), 1))
    pick_y_back = mask(line_of(iota((LANES, ext), 1)), iota((LANES, ext), 0))
    pick_z = mask(level_of(iota((ext, nz), 0)), iota((ext, nz), 1))
    pick_z_back = mask(level_of(iota((nz, ext), 1)), iota((nz, ext), 0))
    own_columns = iota((nz, ext), 1) < all_rows
    _, _, beside = faces(kz_ref[...], nz)
    identity = (iota((nz, nz), 0) == iota((nz, nz), 1)).astype(jnp.float32)
    vertical = beside + identity * (1.0 - jnp.sum(beside, axis=1, keepdims=True))
    for order, (ext_y, mixed) in enumerate(
        ((ext_y_once, vertical), (ext_y_twice, dot(vertical, vertical)))
    ):
        across_y = spread(copied(pick_y, ext_y), pick_y_back)
        levels = jnp.where(own_columns, spread(mixed, pick_z_back), pick_z_back.astype(jnp.float32))
        whole = across_y * copied(pick_z, levels)
        for i, part in enumerate(parts(whole)):
            g_split[order, i] = part
    g_ref[...] = whole
    inner = (my_k * chunk - my_start) * rows

    def inner_rows(r):
        return pl.ds(pl.multiple_of(r * wrows + inner, 8), crows)

    inner_g = jnp.concatenate([g_ref[inner_rows(r), :] for r in range(spots)], axis=0)
    inner_g = jnp.where(iota((spots * crows, ext), 1) < all_rows, inner_g, 0.0)
    for i, part in enumerate(parts(inner_g)):
        g_split[2, i, : spots * crows, :] = part
    q = iota((spots * prows, LANES), 0)
    picked = side * (ny // 2) + (q // prows) * rows + q % rows
    picked = jnp.where(picked == iota((spots * prows, LANES), 1), 1.0, 0.0)[:, :ny]
    enters = [dot(picked, jnp.broadcast_to(c, (ny, LANES))) for c in (enter_twice, enter_once)]
    mix[0] = jnp.where(q % 2 == 0, enters[0], enters[1])
    mix[1] = jnp.where(q % 2 == 0, enters[1], enters[0])

    w_high[:, all_rows:, :] = jnp.zeros((n_tm + 1, ext - all_rows, nx), jnp.bfloat16)
    w_low[:, all_rows:, :] = jnp.zeros((n_tm + 1, ext - all_rows, nx), jnp.bfloat16)

    tile = (iota((nx // TILE, nx), 1) // TILE == iota((nx // TILE, nx), 0)).astype(jnp.float32)
    tiles = nx // TILE
    flags = jnp.where(
        iota((tiles, tiles), 0) == iota((tiles, tiles), 1), sea_ref[...].astype(jnp.float32), 0.0
    )
    sea = jnp.sum(jnp.sum(flags, axis=1, keepdims=True) * tile, axis=0, keepdims=True)

    def gathered(ref, where):
        return jnp.concatenate(
            [ref[where(half)].reshape(all_rows, LANES) for half in range(halves)], axis=1
        )

    def solve_x_lines(n, order, field):
        moved = dot3(parts(field), (a_split[order, 0], a_split[order, 1]))
        w_high[n, :all_rows, :], w_low[n, :all_rows, :] = parts(moved)

    def leaving(n, order, lines):
        padded = 16 * -(-lines // 16)
        block = slice(all_rows, all_rows + padded)
        found = dot3(
            (g_split[order, 0, block, :], g_split[order, 1, block, :]), (w_high[n], w_low[n])
        )
        return found[:lines]

    def joined(n, order):
        w_high[n, all_rows:, :], w_low[n, all_rows:, :] = parts(
            jnp.concatenate(
                [near_in[n], jnp.zeros((ext - all_rows - kept, nx), jnp.float32)], axis=0
            )
        )
        block = slice(0, all_rows)
        return dot3(
            (g_split[order, 0, block, :], g_split[order, 1, block, :]), (w_high[n], w_low[n])
        )

    def slab_of(n):
        return xbuf.at[pl.ds(n * spots, spots)]

    def arrive_u(turned):
        n = here ^ ((turned + 1) % n_tm)

        slot = slab_of(n)
        pltpu.make_async_copy(slot, slot, u_recv.at[n]).wait()
        field = parts(gathered(xbuf, lambda half: (pl.ds(n * spots, spots), half)))
        w_high[n, :all_rows, :], w_low[n, :all_rows, :] = field
        a_twice = a_split[1, 0], a_split[1, 1]
        near_out[n] = dot3(parts(leaving(n, 1, kept)), a_twice)
        send_near(n).start()
        w_high[n, :all_rows, :], w_low[n, :all_rows, :] = parts(dot3(field, a_twice))

    arrive_u(1)

    @pl.loop(1, spots)
    def start_damp(offset):
        send_f(1, offset).start()

    own_f[1].start()

    arrive_u(2)

    pltpu.make_async_copy(dbuf.at[0], dbuf.at[0], f_recv.at[0]).wait()

    source[1] = gathered(dbuf, lambda half: (0, slice(None), half)) * sea
    solve_x_lines(n_tm, 0, source[1])
    near_out[n_tm] = leaving(n_tm, 0, kept)
    send_near(n_tm).start()

    arrive_u(3)
    arrive_u(4)

    pltpu.make_async_copy(qbuf, qbuf, p_recv).wait()
    pltpu.make_async_copy(dbuf.at[1], dbuf.at[1], f_recv.at[1]).wait()

    def wide(values):
        return jnp.concatenate([values[:1]] * halves, axis=1)

    log_damp = jnp.log(gathered(dbuf, lambda half: (1, slice(None), half)))
    product = None
    for n in range(n_tm):
        weight = 1.0 + 0.5 * jnp.cos(2.0 * math.pi * qbuf[n] / PHASES)
        one = jnp.exp(wide(weight) * log_damp)
        factor[n] = one
        product = one if product is None else one * product
    inverse_p[...] = 1.0 / (1.0 - product)

    def wait_near(n):
        pltpu.make_async_copy(near_in.at[n], near_in.at[n], near_recv.at[n]).wait()

    away = xbuf.at[pl.ds(0, count - 1)]
    pltpu.make_async_copy(away, away, u_send).wait()
    away = dbuf.at[:, pl.ds(0, spots - 1)]
    pltpu.make_async_copy(away, away, f_send).wait()
    away = qbuf.at[pl.ds(0, n_tm - 1)]
    pltpu.make_async_copy(away, away, p_send).wait()
    wait_near(n_tm)
    source[0] = joined(n_tm, 0)

    @pl.loop(0, n_tm)
    def make_offsets(n):
        phase = qbuf[n]
        first = jnp.cos(2.0 * math.pi * (phase * STEPS) / (PHASES * STEPS))
        second = jnp.cos(2.0 * math.pi * (phase * STEPS + 1) / (PHASES * STEPS))
        offset_ref[n] = wide(first) * source[0] + wide(second) * source[1]

    @pl.loop(1, n_tm + 1)
    def finish_first(turned):
        n = here ^ ((turned + 1) % n_tm)
        wait_near(n)
        field = gathered(xbuf, lambda half: (pl.ds(n * spots, spots), half))
        state[n] = joined(n, 1) + offset_ref[n] - factor[n] * field

    def solve_first(r):
        block = pl.ds(pl.multiple_of(r * wrows, 8), wrows)
        factors = [factor[n, block, :] for n in range(n_tm)]
        offsets = [state[n, block, :] for n in range(n_tm)]
        total = offsets[0]
        for n in range(1, n_tm):
            total = factors[n] * total + offsets[n]
        fresh = total * inverse_p[block, :]
        for n in range(n_tm):
            state[n, block, :] = fresh
            fresh = factors[n] * fresh + offsets[n]

    for r in range(spots):
        solve_first(r)

    def lanes(half):
        return slice(half * LANES, (half + 1) * LANES)

    first_pieces = 1

    a_twice = a_split[1, 0], a_split[1, 1]
    picked_rows = []
    for n in range(n_tm):
        w_high[n, :all_rows, :], w_low[n, :all_rows, :] = parts(state[n])
        picked_rows.append(leaving(n, 1, tail))
    found = dot3(parts(jnp.concatenate(picked_rows, axis=0)), a_twice)
    for n in range(n_tm):
        for piece, (half, group) in enumerate(pieces):
            first = n * tail + group * prows
            last_out[piece, n] = found[first : first + prows, lanes(half)]
        for piece in range(first_pieces):
            send_last(n, piece).start()

    for piece in range(first_pieces, len(pieces)):

        @pl.loop(0, n_tm)
        def start_last(n):
            send_last(n, piece).start()

    pltpu.make_async_copy(near_in, near_in, near_send).wait()

    def own_last(n):
        upper = slice(0, spots * crows)
        own = dot3(
            (g_split[2, 0, upper, :], g_split[2, 1, upper, :]), (w_high[n], w_low[n])
        )
        own = dot3(parts(own), a_twice)
        for r in range(spots):
            packed = slice(r * crows, (r + 1) * crows)
            block = inner_rows(r)
            ends[n, packed, :] = (
                own[packed] + offset_ref[n, block, :] - factor[n, block, :] * state[n, block, :]
            )

    for n in range(n_tm):
        own_last(n)

    even = iota((prows, LANES), 0) % 2 == 0

    def swapped(a):
        return jnp.where(even, pltpu.roll(a, prows - 1, 0), pltpu.roll(a, 1, 0))

    for piece, (half, group) in enumerate(pieces):
        slot = last_in.at[piece]
        pltpu.make_async_copy(slot, slot, last_recv.at[piece]).wait()

        def solve_last(turned):
            r = (spot + turned) % spots
            block = pl.ds(pl.multiple_of(r * wrows + inner + group * prows, 8), prows)
            packed = pl.ds(pl.multiple_of(r * crows + group * prows, 8), prows)
            mine = pl.ds(pl.multiple_of(r * prows, 8), prows)
            factors = [factor[n, block, lanes(half)] for n in range(n_tm)]
            offsets = []
            for n in range(n_tm):
                entering = last_in[piece, n]
                offsets.append(
                    ends[n, packed, lanes(half)]
                    + mix[0, mine, :] * entering
                    + mix[1, mine, :] * swapped(entering)
                )
            total = offsets[0]
            for n in range(1, n_tm):
                total = factors[n] * total + offsets[n]
            fresh = total * inverse_p[block, lanes(half)]
            for n in range(n_tm):
                obuf[piece * count + n * spots + r] = fresh
                fresh = factors[n] * fresh + offsets[n]
            for n in range(n_tm):

                @pl.when(n * spots + r != me)
                def _():
                    send_o(piece, n * spots + r).start()

        for turned in range(1, spots + 1):
            solve_last(turned)
        pltpu.make_async_copy(obuf.at[piece * count + me], landing(piece), o_recv).start()

    pltpu.make_async_copy(last_in, last_in, last_send).wait()
    pltpu.make_async_copy(out_ref, out_ref, o_recv).wait()
    away = obuf.at[pl.ds(0, len(pieces) * (count - 1))]
    pltpu.make_async_copy(away, away, o_send).wait()


def turn_kernel(size, in_ref, out_ref, near_ref, turned_ref, in_sem, out_sem):
    n_t, halves, rows, nz = size
    blocks = [(t, half) for half in range(halves) for t in range(n_t)]

    def fetch(i):
        return pltpu.make_async_copy(in_ref.at[blocks[i]], near_ref.at[i], in_sem.at[i])

    def store(i):
        t, half = blocks[i]
        place = pl.ds(half * LANES * rows, LANES * rows)
        return pltpu.make_async_copy(turned_ref.at[i], out_ref.at[t, place, :], out_sem.at[i])

    for i in range(len(blocks)):
        fetch(i).start()
    for i in range(len(blocks)):
        fetch(i).wait()
        for y in range(rows):
            part = near_ref[i, pl.ds(y, nz, stride=rows), :]
            turned_ref[i, pl.ds(y, LANES, stride=rows), :] = part.T
        store(i).start()
    for i in range(len(blocks)):
        store(i).wait()


def whole_period(init_states, forcing, damp, kappa_x, kappa_y, kappa_z, sea_tiles, phases):
    n_tm, n_sp = lax.axis_size("tm"), lax.axis_size("space")
    n_t, _, nx, rows, nz = init_states.shape
    spots = n_sp // 2
    count = n_tm * spots
    chunk = nz // (count // n_t)
    window = chunk + 2 * HALO
    halves = nx // LANES
    wrows = window * rows
    crows = chunk * rows
    all_rows = spots * wrows
    kept = 2 * (chunk + HALO)
    prows = crows // GROUPS
    ext = LANES * -(-(all_rows + kept) // LANES)
    flat = (n_t, nx * rows, nz)
    f32 = jnp.float32
    bf16 = jnp.bfloat16
    landed = pl.pallas_call(
        functools.partial(period_kernel, (n_tm, n_sp, n_t, nx, rows, nz)),
        out_shape=jax.ShapeDtypeStruct((n_t, halves, nz * rows, LANES), f32),
        in_specs=[pl.BlockSpec(memory_space=pltpu.HBM)] * 8,
        out_specs=pl.BlockSpec(memory_space=pltpu.HBM),
        scratch_shapes=[
            pltpu.VMEM(flat, f32),
            pltpu.VMEM(flat, f32),
            pltpu.VMEM(flat, f32),
            pltpu.VMEM((1, nx), f32),
            pltpu.VMEM((1, kappa_y.shape[0]), f32),
            pltpu.VMEM((1, nz), f32),
            pltpu.VMEM((1, sea_tiles.shape[0]), jnp.int32),
            pltpu.VMEM((1, 1), jnp.int32),
            pltpu.SemaphoreType.DMA((8,)),
            pltpu.VMEM((all_rows, nx), f32),
            pltpu.VMEM((3, 2, ext, ext), bf16),
            pltpu.VMEM((2, 2, nx, nx), bf16),
            pltpu.VMEM((ext, ext), f32),
            pltpu.VMEM((nx, nx), f32),
            pltpu.VMEM((n_tm + 1, ext, nx), bf16),
            pltpu.VMEM((n_tm + 1, ext, nx), bf16),
            pltpu.VMEM((2, spots * prows, LANES), f32),
            pltpu.VMEM((n_tm, spots * crows, nx), f32),
            pltpu.VMEM((n_t, halves, nz * rows, LANES), f32),
            pltpu.VMEM((n_t, 2, halves, nz * rows, LANES), f32),
            pltpu.VMEM((8, LANES), f32),
            pltpu.VMEM((count, halves, wrows, LANES), f32),
            pltpu.VMEM((2, spots, halves, wrows, LANES), f32),
            pltpu.VMEM((n_tm, 8, LANES), f32),
            pltpu.VMEM((halves * GROUPS * count, prows, LANES), f32),
            pltpu.VMEM((n_tm, all_rows, nx), f32),
            pltpu.VMEM((n_tm, all_rows, nx), f32),
            pltpu.VMEM((2, all_rows, nx), f32),
            pltpu.VMEM((n_tm, all_rows, nx), f32),
            pltpu.VMEM((n_tm + 1, kept, nx), f32),
            pltpu.VMEM((n_tm + 1, kept, nx), f32),
            pltpu.VMEM((halves * GROUPS, n_tm, prows, LANES), f32),
            pltpu.VMEM((halves * GROUPS, n_tm, prows, LANES), f32),
            pltpu.SemaphoreType.DMA,
            pltpu.SemaphoreType.DMA((n_tm,)),
            pltpu.SemaphoreType.DMA,
            pltpu.SemaphoreType.DMA((2,)),
            pltpu.SemaphoreType.DMA,
            pltpu.SemaphoreType.DMA,
            pltpu.SemaphoreType.DMA,
            pltpu.SemaphoreType.DMA,
            pltpu.SemaphoreType.DMA,
            pltpu.SemaphoreType.DMA((n_tm + 1,)),
            pltpu.SemaphoreType.DMA,
            pltpu.SemaphoreType.DMA((halves * GROUPS,)),
        ],
        compiler_params=pltpu.CompilerParams(
            collective_id=0, has_side_effects=True, vmem_limit_bytes=63 * 1024 * 1024
        ),
    )(
        init_states.reshape(flat),
        forcing.reshape(flat),
        damp.reshape(flat),
        kappa_x[None],
        kappa_y[None],
        kappa_z[None],
        sea_tiles.reshape(1, -1),
        phases.reshape(1, 1),
    )
    pieces = n_t * halves
    out = pl.pallas_call(
        functools.partial(turn_kernel, (n_t, halves, rows, nz)),
        out_shape=jax.ShapeDtypeStruct(flat, f32),
        in_specs=[pl.BlockSpec(memory_space=pl.ANY)],
        out_specs=pl.BlockSpec(memory_space=pl.ANY),
        scratch_shapes=[
            pltpu.VMEM((pieces, nz * rows, LANES), f32),
            pltpu.VMEM((pieces, LANES * rows, nz), f32),
            pltpu.SemaphoreType.DMA((pieces,)),
            pltpu.SemaphoreType.DMA((pieces,)),
        ],
    )(landed)
    return out.reshape(init_states.shape)


def choose(init_states, forcing, damp, kappa_x, kappa_y, kappa_z, sea_tiles, phases):
    spots = lax.axis_size("space") // 2
    count = lax.axis_size("tm") * spots
    n_t, slabs, nx, rows, nz = init_states.shape
    ny = lax.axis_size("space") * rows
    per = max(count // n_t, 1)
    chunk = nz // per
    all_rows = spots * (chunk + 2 * HALO) * rows
    fits = (
        ITERS == 2
        and slabs == 1
        and lax.axis_size("space") % 2 == 0
        and lax.axis_size("tm") == 4
        and spots & (spots - 1) == 0
        and count % n_t == 0
        and nz == LANES
        and nx % LANES == 0
        and nz % per == 0
        and rows == 2
        and chunk * rows % (8 * GROUPS) == 0
        and HALO * rows % 8 == 0
        and HALO <= chunk
        and chunk % 8 == 0
        and all_rows % 16 == 0
        and chunk + 2 * HALO <= nz
        and ny + 2 <= LANES
        and ny & (ny - 1) == 0
        and ny >= 16
        and sea_tiles.shape[1] == 1
        and all_rows + 2 * (chunk + HALO) <= 512
    )
    run = whole_period if fits else body
    return run(init_states, forcing, damp, kappa_x, kappa_y, kappa_z, sea_tiles, phases)


def solution(mesh):
    return jax.shard_map(
        choose,
        mesh=mesh,
        in_specs=(
            P(None, "tm", None, "space", None),
            P(None, None, "space", None),
            P(None, None, "space", None),
            P(),
            P(),
            P(),
            P(),
            P("tm"),
        ),
        out_specs=P(None, "tm", None, "space", None),
        check_vma=False,
    )
```
